32 devices in a mesh: dp: 8 (over y, x, core), tensor: 4 (over z).
Axes of the slice: x: 2, y: 2, z: 4, core: 2. Of those that a mesh axis runs over, the one named last changes fastest.
Arguments:
- tokens: bfloat16 [8192, 768], P(('dp', 'tensor')), may hold values from -6 to 6
- cotangent: bfloat16 [8192, 768], P(('dp', 'tensor')), may hold values from -6 to 6
- norm_gain: float32 [2, 2, 768], replicated, may hold values from 0.5 to 1.5
- norm_shift: float32 [2, 2, 768], replicated, may hold values from -3 to 3
- w_qkv: bfloat16 [2, 768, 3, 768], P(None, None, None, 'tensor'), may hold values from -0.3125 to 0.3125
- b_qkv: float32 [2, 3, 768], P(None, None, 'tensor'), may hold values from -3 to 3
- w_out: bfloat16 [2, 768, 768], P(None, 'tensor'), may hold values from -2 to 2
- b_out: float32 [2, 768], replicated, may hold values from -3 to 3
- w_in: bfloat16 [2, 768, 3072], P(None, None, 'tensor'), may hold values from -0.21875 to 0.21875
- b_in: float32 [2, 3072], P(None, 'tensor'), may hold values from -3 to 3
- w_down: bfloat16 [2, 3072, 768], P(None, 'tensor'), may hold values from -0.109375 to 0.109375
- b_down: float32 [2, 768], replicated, may hold values from -3 to 3
Outputs:
- result: float32 [8192, 768], P(('dp', 'tensor'))
- grad_tokens: float32 [8192, 768], P(('dp', 'tensor'))
- grad_norm_gain: float32 [2, 2, 768], replicated
- grad_norm_shift: float32 [2, 2, 768], replicated
- grad_w_qkv: float32 [2, 768, 3, 768], P(None, None, None, 'tensor')
- grad_b_qkv: float32 [2, 3, 768], P(None, None, 'tensor')
- grad_w_out: float32 [2, 768, 768], P(None, 'tensor')
- grad_b_out: float32 [2, 768], replicated
- grad_w_in: float32 [2, 768, 3072], P(None, None, 'tensor')
- grad_b_in: float32 [2, 3072], P(None, 'tensor')
- grad_w_down: float32 [2, 3072, 768], P(None, 'tensor')
- grad_b_down: float32 [2, 768], replicated
The draws below stay inside these ranges and needn't reach their ends.
All inputs are finite; a program needn't handle non-finite values.
Results may differ from the reference program's by a relative error of at most 0.03.
The reference program's roundings to bfloat16 on the way count: a program that leaves them out, or rounds other values in their place, can miss the bound.
Values may be sent and summed in bfloat16 or wider, within the bound.
No kernel may reach another device: no remote copies, remote signals or barrier semaphores. Data moves between devices by JAX's collectives and lax.ppermute only.
A program may use at most 128 MiB of HBM per device.

```python
import math
import jax
import jax.numpy as jnp
from jax import lax

D = 768
HEADS = 12
HD = 64
FF = 3072
ROT = 16
LAYERS = 2
LEN = 1024
TOKENS = 8192


def steps_of(own_key, extent, shards, least, top_value):
    def one(dim, blocks):
        steps = jax.random.uniform(jax.random.fold_in(jax.random.fold_in(own_key, 6), dim), (blocks,), jnp.float32, least / len(shards), top_value / len(shards))
        return jnp.repeat(jnp.exp(steps), extent[dim] // blocks).reshape((-1,) + (1,) * (len(extent) - dim - 1))

    level = one(*shards[0])
    for cut in shards[1:]:
        level = level * one(*cut)
    return level


def noise(own_key, extent, scale, most, pieces=(), held_as=jnp.bfloat16):
    factor_of = steps_of(own_key, extent, pieces, -0.22, 0.18) if pieces else 1.0
    drawn = jax.random.normal(own_key, extent, jnp.float32) * scale * factor_of
    return jnp.minimum(jnp.maximum(drawn, -most), most).astype(held_as)


def setup_inputs(seed: int = 0) -> dict:
    seeds = jax.random.split(jax.random.key(seed), 13)
    tokens = noise(seeds[0], (TOKENS, D), 1.0, 6.0, ((0, 32),))
    cotangent = noise(seeds[1], (TOKENS, D), 1.0, 6.0, ((0, 32),))
    norm_gain = jnp.clip(1.0 + 0.1 * jax.random.normal(seeds[2], (LAYERS, 2, D), jnp.float32), 0.5, 1.5)
    norm_shift = noise(seeds[3], (LAYERS, 2, D), 0.5, 3.0, (), jnp.float32)
    w_qkv = noise(seeds[4], (LAYERS, D, 3, D), (D // 2) ** -0.5, 0.3125, ((3, 4),))
    b_qkv = noise(seeds[5], (LAYERS, 3, D), 0.5, 3.0, ((2, 4),), jnp.float32)
    w_out = noise(seeds[6], (LAYERS, D, D), 8 ** -0.5, 2.0, ((1, 4),))
    b_out = noise(seeds[7], (LAYERS, D), 0.5, 3.0, (), jnp.float32)
    w_in = noise(seeds[8], (LAYERS, D, FF), D ** -0.5, 0.21875, ((2, 4),))
    b_in = noise(seeds[9], (LAYERS, FF), 0.5, 3.0, ((1, 4),), jnp.float32)
    w_down = noise(seeds[10], (LAYERS, FF, D), FF ** -0.5, 0.109375, ((1, 4),))
    b_down = noise(seeds[11], (LAYERS, D), 0.5, 3.0, (), jnp.float32)
    return {"tokens": tokens, "cotangent": cotangent, "norm_gain": norm_gain, "norm_shift": norm_shift, "w_qkv": w_qkv, "b_qkv": b_qkv, "w_out": w_out, "b_out": b_out, "w_in": w_in, "b_in": b_in, "w_down": w_down, "b_down": b_down}


@jax.custom_vjp
def low(v):
    return lax.optimization_barrier(v.astype(jnp.bfloat16)).astype(jnp.float32)

@jax.custom_vjp
def low_back(v):
    return v

def low_keep(v):
    return (low(v), None)

def low_pass(kept, grad):
    return (grad,)

def back_keep(v):
    return (v, None)

def back_low(kept, grad):
    return (low(grad),)
low.defvjp(low_keep, low_pass)
low_back.defvjp(back_keep, back_low)
epsilon = 1e-05
highest = lax.Precision.HIGHEST

def layer_norm(rows, gain, shift):
    centre = rows - lax.optimization_barrier(jnp.mean(rows, axis=-1, keepdims=True))
    spread = lax.optimization_barrier(jnp.mean(centre * centre, axis=-1, keepdims=True))
    return centre * lax.rsqrt(spread + epsilon) * gain + shift

def rotary_tables(count):
    half = ROT // 2
    places = (jnp.arange(count, dtype=jnp.int32) % LEN).astype(jnp.float32)
    freqs = jnp.exp(jnp.arange(half, dtype=jnp.float32) * (-2.0 * math.log(10000.0) / ROT))
    angles = places[:, None] * freqs[None, :]
    return (jnp.cos(angles)[:, None, :], jnp.sin(angles)[:, None, :])

def rotate(values, cosine, sine):
    half = ROT // 2
    first = values[..., :half]
    second = values[..., half:ROT]
    return jnp.concatenate([first * cosine - second * sine, second * cosine + first * sine, values[..., ROT:]], axis=-1)

def gelu_exact(values):
    return jax.nn.gelu(values, approximate=False)

def attend(inputs):
    query, key, value = inputs
    scale = HD ** (-0.5)
    scores = low_back(jnp.einsum('qhd,khd->hqk', query, key, precision=highest) * scale)
    causal = jnp.arange(LEN)[None, :] <= jnp.arange(LEN)[:, None]
    scores = jnp.where(causal[None], scores, -1e+30)
    top = lax.optimization_barrier(jnp.max(scores, axis=-1, keepdims=True))
    weights = jnp.exp(scores - top)
    probs = low(weights / lax.optimization_barrier(jnp.sum(weights, axis=-1, keepdims=True)))
    return jnp.einsum('hqk,khd->qhd', probs, value, precision=highest)

def forward(stream, gains, shifts, wqkv, bqkv, wout, bout, win, bin_, wdown, bdown):
    count = stream.shape[0]
    seq_count = count // LEN
    cosine, sine = rotary_tables(count)
    for layer_index in range(LAYERS):
        attn_in = low(layer_norm(stream, gains[layer_index, 0], shifts[layer_index, 0]))
        mlp_in = low(layer_norm(stream, gains[layer_index, 1], shifts[layer_index, 1]))
        projected = low_back(jnp.einsum('td,dcf->tcf', attn_in, wqkv[layer_index], precision=highest) + bqkv[layer_index])
        split = projected.reshape(count, 3, HEADS, HD)
        query = low(rotate(split[:, 0], cosine, sine))
        key = low(rotate(split[:, 1], cosine, sine))
        value = low(split[:, 2])
        shaped = (query.reshape(seq_count, LEN, HEADS, HD), key.reshape(seq_count, LEN, HEADS, HD), value.reshape(seq_count, LEN, HEADS, HD))
        mixed = lax.map(jax.checkpoint(attend), shaped)
        mixed = low_back(low(mixed.reshape(count, D)))
        hidden_pre = low_back(jnp.dot(mlp_in, win[layer_index], precision=highest) + bin_[layer_index])
        hidden = low(gelu_exact(hidden_pre))
        branch = low_back(jnp.dot(mixed, wout[layer_index], precision=highest) + bout[layer_index] + jnp.dot(hidden, wdown[layer_index], precision=highest) + bdown[layer_index])
        stream = stream + branch
    return stream

def reference(tokens, cotangent, norm_gain, norm_shift, w_qkv, b_qkv, w_out, b_out, w_in, b_in, w_down, b_down):
    inputs = (tokens.astype(jnp.float32), norm_gain, norm_shift, w_qkv.astype(jnp.float32), b_qkv, w_out.astype(jnp.float32), b_out, w_in.astype(jnp.float32), b_in, w_down.astype(jnp.float32), b_down)
    result, pull = jax.vjp(forward, *inputs)
    grads = pull(cotangent.astype(jnp.float32))
    return (result, grads[0], grads[1], grads[2], grads[3], grads[4], grads[5], grads[6], grads[7], grads[8], grads[9], grads[10])
```

```python
import functools
import math

import jax
import jax.numpy as jnp
from jax import lax
from jax.experimental import pallas as pl
from jax.experimental.pallas import tpu as pltpu
from jax.sharding import PartitionSpec as P

HD = 64
ROT = 16
LEN = 1024
EPS = 1e-05
BF = jnp.bfloat16
F32 = jnp.float32
NEG = -1e30
ROWS = 256
MIB = 1024 * 1024


def dot(a, b, ca, cb):
    return lax.dot_general(a, b, (((ca,), (cb,)), ((), ())), preferred_element_type=F32)


def normalize(rows):
    centre = rows - jnp.mean(rows, axis=-1, keepdims=True)
    scale = lax.rsqrt(jnp.mean(centre * centre, axis=-1, keepdims=True) + EPS)
    return centre * scale, scale


def rope_tables(sign):
    half = ROT // 2
    places = jnp.arange(LEN, dtype=jnp.int32).astype(F32)
    freqs = jnp.exp(jnp.arange(half, dtype=F32) * (-2.0 * math.log(10000.0) / ROT))
    angles = places[:, None] * freqs[None, :]
    cosine, sine = jnp.cos(angles), jnp.sin(angles) * sign
    rest = HD - ROT
    zeros = jnp.zeros_like(sine)
    wide = jnp.zeros((LEN, rest), F32)
    c = jnp.concatenate([cosine, cosine, wide + 1.0], axis=1)
    s_left = jnp.concatenate([-sine, zeros, wide], axis=1)
    s_right = jnp.concatenate([zeros, sine, wide], axis=1)
    return jnp.stack([jnp.concatenate([t, t], axis=1) for t in (c, s_left, s_right)])


def turn(group, tables):
    return (
        group * tables[0]
        + pltpu.roll(group, 128 - ROT // 2, 1) * tables[1]
        + pltpu.roll(group, ROT // 2, 1) * tables[2]
    )


def project_kernel(
    is_raw, x_ref, gain_ref, shift_ref, table_ref, wqkv_ref, bqkv_ref, win_ref, bin_ref,
    attn_ref, mlp_ref, qkv_ref, hidden_ref, slope_ref,
):
    x = x_ref[...].astype(F32)
    n = normalize(x)[0] if is_raw else x
    attn_in = (n * gain_ref[0:1] + shift_ref[0:1]).astype(BF)
    mlp_in = (n * gain_ref[1:2] + shift_ref[1:2]).astype(BF)
    attn_ref[...] = attn_in
    mlp_ref[...] = mlp_in
    projected = dot(attn_in, wqkv_ref[...], 1, 1) + bqkv_ref[...]
    part = projected.shape[1] // 3
    heads = part // HD
    tables = table_ref[...]
    pieces = []
    for g in range(2 * part // 128):
        pieces.append(turn(projected[:, g * 128 : (g + 1) * 128], tables).astype(BF))
    rotated = jnp.concatenate(pieces, axis=1)
    for i in range(2 * heads):
        qkv_ref[i] = rotated[:, i * HD : (i + 1) * HD]
    value = projected[:, 2 * part :].astype(BF)
    for i in range(heads):
        qkv_ref[2 * heads + i] = value[:, i * HD : (i + 1) * HD]
    pre = dot(mlp_in, win_ref[...], 1, 0) + bin_ref[...]
    phi = 0.5 * (1.0 + lax.erf(pre * (1.0 / math.sqrt(2.0))))
    hidden_ref[...] = (pre * phi).astype(BF)
    slope_ref[...] = phi + pre * jnp.exp(-0.5 * pre * pre) * (1.0 / math.sqrt(2.0 * math.pi))


def project(x, is_raw, gains, shifts, tables, wqkv, bqkv, win, bin_):
    count, width = x.shape
    qkv_width, ff = wqkv.shape[0], win.shape[1]
    parts = qkv_width // HD
    whole = lambda *shape: pl.BlockSpec(shape, lambda i: (0,) * len(shape))
    rows = lambda w: pl.BlockSpec((ROWS, w), lambda i: (i, 0))
    per_seq = LEN // ROWS
    return pl.pallas_call(
        functools.partial(project_kernel, is_raw),
        grid=(count // ROWS,),
        in_specs=[
            rows(width), whole(2, width), whole(2, width),
            pl.BlockSpec((3, ROWS, 128), lambda i: (0, i % per_seq, 0)),
            whole(qkv_width, width), whole(1, qkv_width), whole(width, ff), whole(1, ff),
        ],
        out_specs=[
            rows(width), rows(width),
            pl.BlockSpec((parts, ROWS, HD), lambda i: (0, i, 0)),
            rows(ff), rows(ff),
        ],
        out_shape=[
            jax.ShapeDtypeStruct((count, width), BF),
            jax.ShapeDtypeStruct((count, width), BF),
            jax.ShapeDtypeStruct((parts, count, HD), BF),
            jax.ShapeDtypeStruct((count, ff), BF),
            jax.ShapeDtypeStruct((count, ff), F32),
        ],
        compiler_params=pltpu.CompilerParams(vmem_limit_bytes=32 * MIB),
        cost_estimate=pl.CostEstimate(
            flops=2 * count * width * (qkv_width + ff), bytes_accessed=12 * MIB, transcendentals=2 * count * ff
        ),
        name="project",
    )(x, gains, shifts, tables, wqkv, bqkv.reshape(1, -1), win, bin_.reshape(1, -1))


def attend_kernel(qkv_ref, mixed_ref):
    heads = qkv_ref.shape[0] // 3
    row = lax.broadcasted_iota(jnp.int32, (ROWS, ROWS), 0)
    col = lax.broadcasted_iota(jnp.int32, (ROWS, ROWS), 1)
    allowed = col <= row
    for h in range(heads):
        for b in range(LEN // ROWS):
            lo, hi = b * ROWS, (b + 1) * ROWS
            q = (qkv_ref[h, lo:hi].astype(F32) * HD ** (-0.5)).astype(BF)
            s = dot(q, qkv_ref[heads + h, 0:hi], 1, 1)
            edge = jnp.where(allowed, s[:, lo:hi], NEG)
            s = edge if b == 0 else jnp.concatenate([s[:, :lo], edge], axis=1)
            e = jnp.exp(s - jnp.max(s, axis=1, keepdims=True))
            p = (e * (1.0 / jnp.sum(e, axis=1, keepdims=True))).astype(BF)
            o = dot(p, qkv_ref[2 * heads + h, 0:hi], 1, 0)
            mixed_ref[lo:hi, h * HD : (h + 1) * HD] = o.astype(BF)


def attend(qkv):
    parts, count, _ = qkv.shape
    heads = parts // 3
    return pl.pallas_call(
        attend_kernel,
        grid=(count // LEN,),
        in_specs=[pl.BlockSpec((parts, LEN, HD), lambda i: (0, i, 0))],
        out_specs=pl.BlockSpec((LEN, heads * HD), lambda i: (i, 0)),
        out_shape=jax.ShapeDtypeStruct((count, heads * HD), BF),
        compiler_params=pltpu.CompilerParams(vmem_limit_bytes=32 * MIB),
        cost_estimate=pl.CostEstimate(
            flops=8 * count * LEN * HD * heads, bytes_accessed=4 * MIB, transcendentals=count * LEN * heads
        ),
        name="attend",
    )(qkv)


def attend_back_kernel(qkv_ref, grad_ref, wout_ref, table_ref, out_ref, gm_ref, dq_ref, dk_ref, dv_ref):
    heads = qkv_ref.shape[0] // 3
    part = heads * HD
    for b in range(LEN // ROWS):
        lo, hi = b * ROWS, (b + 1) * ROWS
        gm = dot(grad_ref[lo:hi], wout_ref[...], 1, 1).astype(BF)
        for h in range(heads):
            gm_ref[h, lo:hi] = gm[:, h * HD : (h + 1) * HD]
    row = lax.broadcasted_iota(jnp.int32, (ROWS, ROWS), 0)
    col = lax.broadcasted_iota(jnp.int32, (ROWS, ROWS), 1)
    allowed = row <= col
    scale = HD ** (-0.5)
    blocks = LEN // ROWS
    for h in range(heads):
        for b in reversed(range(blocks)):
            lo, hi = b * ROWS, (b + 1) * ROWS
            q = (qkv_ref[h, lo:hi].astype(F32) * scale).astype(BF)
            key = qkv_ref[heads + h, 0:hi]
            s = dot(key, q, 1, 1)
            edge = jnp.where(allowed, s[lo:hi], NEG)
            s = edge if b == 0 else jnp.concatenate([s[:lo], edge], axis=0)
            e = jnp.exp(s - jnp.max(s, axis=0, keepdims=True))
            p = e * (1.0 / jnp.sum(e, axis=0, keepdims=True))
            gm = gm_ref[h, lo:hi]
            dv = dot(p.astype(BF), gm, 1, 0)
            dp = dot(qkv_ref[2 * heads + h, 0:hi], gm, 1, 1)
            delta = jnp.sum(p * dp, axis=0, keepdims=True)
            ds = (p * (dp - delta)).astype(BF)
            dk = dot(ds, q, 1, 0)
            dq = dot(ds, key, 0, 0) * scale
            dq_ref[lo:hi, h * HD : (h + 1) * HD] = dq
            if b == blocks - 1:
                dk_ref[...] = dk
                dv_ref[...] = dv
            else:
                dk_ref[0:hi] += dk
                dv_ref[0:hi] += dv
        dq_ref[:, part + h * HD : part + (h + 1) * HD] = dk_ref[...]
        out_ref[:, 2 * part + h * HD : 2 * part + (h + 1) * HD] = dv_ref[...].astype(BF)
    tables = table_ref[...]
    for g in range(2 * part // 128):
        lanes = slice(g * 128, (g + 1) * 128)
        out_ref[:, lanes] = turn(dq_ref[:, lanes], tables).astype(BF)


def attend_back(qkv, grad_all, wout, tables):
    parts, count, _ = qkv.shape
    heads = parts // 3
    width = grad_all.shape[1]
    part = heads * HD
    return pl.pallas_call(
        attend_back_kernel,
        grid=(count // LEN,),
        in_specs=[
            pl.BlockSpec((parts, LEN, HD), lambda i: (0, i, 0)),
            pl.BlockSpec((LEN, width), lambda i: (i, 0)),
            pl.BlockSpec((part, width), lambda i: (0, 0)),
            pl.BlockSpec((3, LEN, 128), lambda i: (0, 0, 0)),
        ],
        out_specs=pl.BlockSpec((LEN, 3 * part), lambda i: (i, 0)),
        out_shape=jax.ShapeDtypeStruct((count, 3 * part), BF),
        scratch_shapes=[
            pltpu.VMEM((heads, LEN, HD), BF),
            pltpu.VMEM((LEN, 2 * part), F32),
            pltpu.VMEM((LEN, HD), F32),
            pltpu.VMEM((LEN, HD), F32),
        ],
        compiler_params=pltpu.CompilerParams(vmem_limit_bytes=40 * MIB),
        cost_estimate=pl.CostEstimate(
            flops=20 * count * LEN * HD * heads, bytes_accessed=8 * MIB, transcendentals=count * LEN * heads
        ),
        name="attend_back",
    )(qkv, grad_all, wout, tables)


UP = [(0, 1), (1, 2), (2, 3)]
DOWN = [(1, 0), (2, 1), (3, 2)]


def send(x, pairs):
    return lax.ppermute(x, "tensor", pairs)


def gather_rows(x):
    if lax.axis_size("tensor") != 4:
        return lax.all_gather(x, "tensor", axis=0, tiled=True)
    i = lax.axis_index("tensor")
    below, above = send(x, UP), send(x, DOWN)
    a = send(above, [(1, 0), (2, 1)])
    b = send(above, [(2, 0)])
    c = send(below, [(2, 3), (1, 2)])
    d = send(below, [(1, 3)])
    pick = lambda *four: lax.select_n(jnp.broadcast_to(i, x.shape), *four)
    return jnp.concatenate(
        [pick(x, below, c, d), pick(above, x, below, c), pick(a, above, x, below), pick(b, a, above, x)], axis=0
    )


def scatter_sum(x):
    if lax.axis_size("tensor") != 4:
        return lax.psum_scatter(x, "tensor", scatter_dimension=0, tiled=True).astype(F32)
    i = lax.axis_index("tensor")
    rows = x.shape[0] // 4
    own = lambda k: lax.dynamic_slice_in_dim(x, jnp.clip(i + k, 0, 3) * rows, rows, 0)
    a = send(own(2), [(0, 1), (1, 2)])
    b = send(own(3), [(0, 2)])
    c = send(own(-2), [(3, 2), (2, 1)])
    d = send(own(-3), [(3, 1)])
    total = lambda *terms: sum(t.astype(F32) for t in terms)
    from_above = send(total(own(-1), c, d).astype(BF), DOWN)
    from_below = send(total(own(1), a, b).astype(BF), UP)
    return total(own(0), from_above, from_below)


def partner(x, axis, bit):
    return lax.ppermute(x, axis, [(k, k ^ bit) for k in range(lax.axis_size(axis))])


def halve(x, bit):
    side = (lax.axis_index("dp") // bit) % 2
    half = x.shape[0] // 2
    mine = lax.dynamic_slice_in_dim(x, side * half, half, 0)
    other = lax.dynamic_slice_in_dim(x, (1 - side) * half, half, 0)
    return (mine.astype(F32) + partner(other, "dp", bit).astype(F32)).astype(BF)


def unhalve(x, bit):
    side = (lax.axis_index("dp") // bit) % 2
    got = partner(x, "dp", bit)
    return jnp.concatenate([jnp.where(side == 0, x, got), jnp.where(side == 0, got, x)], axis=0)


def sum_dp(x):
    size = lax.axis_size("dp")
    if size % 8 or x.shape[0] % 256:
        return lax.psum(x, "dp")
    y = halve(x, 1)
    half = y.shape[0] // 2
    a, b = halve(halve(y[:half], 2), 4), halve(halve(y[half:], 4), 2)
    if size > 8:
        groups = [[g * 8 + k for g in range(size // 8)] for k in range(8)]
        a, b = lax.psum((a, b), "dp", axis_index_groups=groups)
    a, b = unhalve(unhalve(a, 4), 2), unhalve(unhalve(b, 2), 4)
    return unhalve(jnp.concatenate([a, b], axis=0), 1)


def sum_small(x, axis):
    size = lax.axis_size(axis)
    if size & (size - 1):
        return lax.psum(x, axis)
    bit = 1
    while bit < size:
        x = x + partner(x, axis, bit)
        bit *= 2
    return x


def body(tokens, cotangent, norm_gain, norm_shift, w_qkv, b_qkv, w_out, b_out, w_in, b_in, w_down, b_down):
    layers = w_qkv.shape[0]
    width = tokens.shape[1]
    ff = w_in.shape[2]
    wqkv = w_qkv.transpose(0, 2, 3, 1).reshape(layers, -1, width)
    tables, tables_back = rope_tables(1.0), rope_tables(-1.0)

    stream = tokens.astype(F32)
    gathered = gather_rows(tokens)
    grad_all = gather_rows(cotangent)
    kept = []
    for l in range(layers):
        n_own, scale = normalize(stream)
        if l > 0:
            gathered = gather_rows(n_own.astype(BF))
        attn_in, mlp_in, qkv, hidden, slope = project(
            gathered, l == 0, norm_gain[l], norm_shift[l], tables, wqkv[l], b_qkv[l], w_in[l], b_in[l]
        )
        mixed = attend(qkv)
        branch = (dot(mixed, w_out[l], 1, 0) + dot(hidden, w_down[l], 1, 0)).astype(BF)
        kept.append((n_own, scale, gathered, attn_in, mlp_in, qkv, hidden, slope, mixed))
        stream = stream + scatter_sum(branch) + b_out[l] + b_down[l]

    grad_stream = cotangent.astype(F32)
    big, biases, norms = [None] * layers, [None] * layers, [None] * layers
    for l in reversed(range(layers)):
        n_own, scale, gathered, attn_in, mlp_in, qkv, hidden, slope, mixed = kept[l]
        if l < layers - 1:
            grad_all = gather_rows(grad_stream.astype(BF))
        grad_hidden = dot(grad_all, w_down[l], 1, 1)
        grad_pre = (grad_hidden * slope).astype(BF)
        grad_projected = attend_back(qkv, grad_all, w_out[l], tables_back)
        grad_mlp = dot(grad_pre, w_in[l], 1, 1)
        grad_attn = dot(grad_projected, wqkv[l], 1, 0)
        h = (grad_attn * norm_gain[l, 0] + grad_mlp * norm_gain[l, 1]).astype(BF)
        h_own = scatter_sum(h)
        n_all = normalize(gathered.astype(F32))[0] if l == 0 else gathered.astype(F32)
        norms[l] = jnp.stack(
            [jnp.sum(grad_attn * n_all, 0), jnp.sum(grad_mlp * n_all, 0), jnp.sum(grad_attn, 0), jnp.sum(grad_mlp, 0)]
        )
        biases[l] = (
            jnp.sum(grad_projected.astype(F32), 0), jnp.sum(grad_pre.astype(F32), 0), jnp.sum(grad_all.astype(F32), 0)
        )
        weights = [
            dot(grad_projected, attn_in, 0, 0),
            dot(mixed, grad_all, 0, 0),
            dot(mlp_in, grad_pre, 0, 0),
            dot(hidden, grad_all, 0, 0),
        ]
        packed = jnp.concatenate([w.astype(BF) for w in weights], axis=0)
        big[l] = sum_dp(packed)
        grad_stream = grad_stream + scale * (
            h_own
            - jnp.mean(h_own, axis=-1, keepdims=True)
            - n_own * jnp.mean(h_own * n_own, axis=-1, keepdims=True)
        )

    norm_sums = sum_small(jnp.concatenate(norms, axis=0), "tensor")
    flat = [norm_sums.reshape(-1)] + [v for three in biases for v in three]
    sizes = [v.shape[0] for v in flat]
    small = sum_small(jnp.concatenate(flat).reshape(-1, 128), "dp").reshape(-1)
    pieces = jnp.split(small, [sum(sizes[: k + 1]) for k in range(len(sizes) - 1)])
    norm_sums = pieces[0].reshape(layers, 4, width)
    part = wqkv.shape[1]
    fo = w_out.shape[1]
    grads = jnp.stack(big).astype(F32)
    g_qkv = grads[:, :part].reshape(layers, 3, part // 3, width).transpose(0, 3, 1, 2)
    g_out = grads[:, part : part + fo]
    g_in = grads[:, part + fo : part + fo + width]
    g_down = grads[:, part + fo + width :]
    gb_qkv = jnp.stack([pieces[1 + 3 * l] for l in range(layers)]).reshape(layers, 3, part // 3)
    gb_in = jnp.stack([pieces[2 + 3 * l] for l in range(layers)])
    gb_out = jnp.stack([pieces[3 + 3 * l] for l in range(layers)])
    return (
        stream, grad_stream, norm_sums[:, 0:2], norm_sums[:, 2:4],
        g_qkv, gb_qkv, g_out, gb_out, g_in, gb_in, g_down, gb_out,
    )


def solution(mesh):
    rows = P(("dp", "tensor"), None)
    specs = (
        P(None, None, None, "tensor"), P(None, None, "tensor"), P(None, "tensor", None), P(),
        P(None, None, "tensor"), P(None, "tensor"), P(None, "tensor", None), P(),
    )
    both = (rows, rows, P(), P()) + specs
    return jax.shard_map(body, mesh=mesh, in_specs=both, out_specs=both, check_vma=False)
```

```python
import functools
import math

import jax
import jax.numpy as jnp
from jax import lax
from jax.experimental import pallas as pl
from jax.experimental.pallas import tpu as pltpu
from jax.sharding import PartitionSpec as P

HD = 64
ROT = 16
LEN = 1024
EPS = 1e-05
BF = jnp.bfloat16
F32 = jnp.float32
NEG = -1e30
ROWS = 256
MIB = 1024 * 1024


def dot(a, b, ca, cb):
    return lax.dot_general(a, b, (((ca,), (cb,)), ((), ())), preferred_element_type=F32)


def normalize(rows):
    centre = rows - jnp.mean(rows, axis=-1, keepdims=True)
    scale = lax.rsqrt(jnp.mean(centre * centre, axis=-1, keepdims=True) + EPS)
    return centre * scale, scale


def rope_tables():
    half = ROT // 2
    lane = jnp.arange(128, dtype=jnp.int32) % HD
    places = jnp.arange(LEN, dtype=jnp.int32).astype(F32)
    freqs = jnp.exp((lane % half).astype(F32) * (-2.0 * math.log(10000.0) / ROT))
    angles = places[:, None] * freqs[None, :]
    cosine = jnp.where(lane < ROT, jnp.cos(angles), 1.0)
    sine = jnp.sin(angles)
    left = jnp.where(lane < half, -sine, 0.0)
    right = jnp.where((lane >= half) & (lane < ROT), sine, 0.0)
    return jnp.stack([cosine, left, right])


def turn(group, tables, sign):
    swung = pltpu.roll(group, 128 - ROT // 2, 1) * tables[1] + pltpu.roll(group, ROT // 2, 1) * tables[2]
    return group * tables[0] + swung if sign > 0 else group * tables[0] - swung


def project_kernel(
    is_raw, x_ref, gain_ref, shift_ref, table_ref, wqkv_ref, bqkv_ref, win_ref, bin_ref,
    attn_ref, mlp_ref, qkv_ref, hidden_ref, slope_ref,
):
    x = x_ref[...].astype(F32)
    n = normalize(x)[0] if is_raw else x
    attn_in = (n * gain_ref[0:1] + shift_ref[0:1]).astype(BF)
    mlp_in = (n * gain_ref[1:2] + shift_ref[1:2]).astype(BF)
    attn_ref[...] = attn_in
    mlp_ref[...] = mlp_in
    projected = dot(attn_in, wqkv_ref[...], 1, 1) + bqkv_ref[...]
    part = projected.shape[1] // 3
    heads = part // HD
    tables = table_ref[...]
    pieces = []
    for g in range(2 * part // 128):
        pieces.append(turn(projected[:, g * 128 : (g + 1) * 128], tables, 1).astype(BF))
    rotated = jnp.concatenate(pieces, axis=1)
    for i in range(2 * heads):
        qkv_ref[i] = rotated[:, i * HD : (i + 1) * HD]
    value = projected[:, 2 * part :].astype(BF)
    for i in range(heads):
        qkv_ref[2 * heads + i] = value[:, i * HD : (i + 1) * HD]
    pre = dot(mlp_in, win_ref[...], 1, 0) + bin_ref[...]
    phi = 0.5 * (1.0 + lax.erf(pre * (1.0 / math.sqrt(2.0))))
    hidden_ref[...] = (pre * phi).astype(BF)
    slope_ref[...] = phi + pre * jnp.exp(-0.5 * pre * pre) * (1.0 / math.sqrt(2.0 * math.pi))


def whole(*shape):
    return pl.BlockSpec(shape, lambda *g: (0,) * len(shape))


def project(x, is_raw, gains, shifts, tables, wqkv, bqkv, win, bin_):
    count, width = x.shape
    qkv_width, ff = wqkv.shape[0], win.shape[1]
    parts = qkv_width // HD
    rows = lambda w: pl.BlockSpec((ROWS, w), lambda i: (i, 0))
    return pl.pallas_call(
        functools.partial(project_kernel, is_raw),
        grid=(count // ROWS,),
        in_specs=[rows(width), whole(2, width), whole(2, width), pl.BlockSpec((3, ROWS, 128), lambda i: (0, i, 0))]
        + [whole(qkv_width, width), whole(1, qkv_width), whole(width, ff), whole(1, ff)],
        out_specs=[
            rows(width), rows(width),
            pl.BlockSpec((parts, ROWS, HD), lambda i: (0, i, 0)),
            rows(ff), rows(ff),
        ],
        out_shape=[
            jax.ShapeDtypeStruct((count, width), BF),
            jax.ShapeDtypeStruct((count, width), BF),
            jax.ShapeDtypeStruct((parts, count, HD), BF),
            jax.ShapeDtypeStruct((count, ff), BF),
            jax.ShapeDtypeStruct((count, ff), F32),
        ],
        compiler_params=pltpu.CompilerParams(vmem_limit_bytes=32 * MIB),
        cost_estimate=pl.CostEstimate(
            flops=2 * count * width * (qkv_width + ff), bytes_accessed=12 * MIB, transcendentals=2 * count * ff
        ),
        name="project",
    )(x, gains, shifts, tables, wqkv, bqkv.reshape(1, -1), win, bin_.reshape(1, -1))


def attend_kernel(which_ref, qkv_ref, hidden_ref, wout_ref, wdown_ref, out_ref, mixed_ref):
    heads = qkv_ref.shape[0] // 3
    step = pl.program_id(0)
    block = which_ref[step]
    row = lax.broadcasted_iota(jnp.int32, (ROWS, ROWS), 0)
    col = lax.broadcasted_iota(jnp.int32, (ROWS, ROWS), 1)
    allowed = col <= row
    for b in range(LEN // ROWS):

        @pl.when(block == b)
        def _(b=b):
            lo, hi = b * ROWS, (b + 1) * ROWS
            for h in range(heads):
                q = (qkv_ref[h, lo:hi].astype(F32) * HD ** (-0.5)).astype(BF)
                s = dot(q, qkv_ref[heads + h, 0:hi], 1, 1)
                edge = jnp.where(allowed, s[:, lo:hi], NEG)
                s = edge if b == 0 else jnp.concatenate([s[:, :lo], edge], axis=1)
                e = jnp.exp(s - jnp.max(s, axis=1, keepdims=True))
                p = (e * (1.0 / jnp.sum(e, axis=1, keepdims=True))).astype(BF)
                o = dot(p, qkv_ref[2 * heads + h, 0:hi], 1, 0)
                mixed_ref[:, h * HD : (h + 1) * HD] = o.astype(BF)

    branch = dot(mixed_ref[...], wout_ref[...], 1, 0) + dot(hidden_ref[...], wdown_ref[...], 1, 0)
    out_ref[...] = branch.astype(BF)


def attend(which, qkv, hidden, wout, wdown):
    parts, count, _ = qkv.shape
    slots = which.shape[0]
    part, width = wout.shape
    ff = wdown.shape[0]
    rows = lambda w: pl.BlockSpec((ROWS, w), lambda g, ref: (ref[g], 0))
    return pl.pallas_call(
        attend_kernel,
        grid_spec=pltpu.PrefetchScalarGridSpec(
            num_scalar_prefetch=1,
            grid=(slots,),
            in_specs=[whole(parts, count, HD), rows(ff), whole(part, width), whole(ff, width)],
            out_specs=[rows(width), rows(part)],
        ),
        out_shape=[jax.ShapeDtypeStruct((count, width), BF), jax.ShapeDtypeStruct((count, part), BF)],
        compiler_params=pltpu.CompilerParams(vmem_limit_bytes=32 * MIB),
        cost_estimate=pl.CostEstimate(
            flops=8 * slots * ROWS * LEN * part, bytes_accessed=4 * MIB, transcendentals=slots * ROWS * LEN * parts // 3
        ),
        name="attend",
    )(which, qkv, hidden, wout, wdown)


def attend_back_kernel(qkv_ref, grad_ref, wout_ref, table_hbm, *refs):
    out_ref, gm_ref, dq_ref, dk_ref, dv_ref, table_ref, sem = refs[-7:]
    heads = qkv_ref.shape[0] // 3
    part = heads * HD
    fetch = pltpu.make_async_copy(table_hbm, table_ref, sem)
    fetch.start()
    for b in range(LEN // ROWS):
        lo, hi = b * ROWS, (b + 1) * ROWS
        gm = dot(grad_ref[lo:hi], wout_ref[...], 1, 1).astype(BF)
        for h in range(heads):
            gm_ref[h, lo:hi] = gm[:, h * HD : (h + 1) * HD]
    row = lax.broadcasted_iota(jnp.int32, (ROWS, ROWS), 0)
    col = lax.broadcasted_iota(jnp.int32, (ROWS, ROWS), 1)
    allowed = row <= col
    scale = HD ** (-0.5)
    blocks = LEN // ROWS
    for h in range(heads):
        for b in reversed(range(blocks)):
            lo, hi = b * ROWS, (b + 1) * ROWS
            q = (qkv_ref[h, lo:hi].astype(F32) * scale).astype(BF)
            key = qkv_ref[heads + h, 0:hi]
            s = dot(key, q, 1, 1)
            edge = jnp.where(allowed, s[lo:hi], NEG)
            s = edge if b == 0 else jnp.concatenate([s[:lo], edge], axis=0)
            e = jnp.exp(s - jnp.max(s, axis=0, keepdims=True))
            p = e * (1.0 / jnp.sum(e, axis=0, keepdims=True))
            gm = gm_ref[h, lo:hi]
            dv = dot(p.astype(BF), gm, 1, 0)
            dp = dot(qkv_ref[2 * heads + h, 0:hi], gm, 1, 1)
            delta = jnp.sum(p * dp, axis=0, keepdims=True)
            ds = (p * (dp - delta)).astype(BF)
            dk = dot(ds, q, 1, 0)
            dq = dot(ds, key, 0, 0) * scale
            dq_ref[lo:hi, h * HD : (h + 1) * HD] = dq
            if b == blocks - 1:
                dk_ref[...] = dk
                dv_ref[...] = dv
            else:
                dk_ref[0:hi] += dk
                dv_ref[0:hi] += dv
        dq_ref[:, part + h * HD : part + (h + 1) * HD] = dk_ref[...]
        out_ref[:, 2 * part + h * HD : 2 * part + (h + 1) * HD] = dv_ref[...].astype(BF)
    fetch.wait()
    tables = table_ref[...]
    for g in range(2 * part // 128):
        lanes = slice(g * 128, (g + 1) * 128)
        out_ref[:, lanes] = turn(dq_ref[:, lanes], tables, -1).astype(BF)


def attend_back(qkv, grad_all, wout, tables, *first):
    parts, count, _ = qkv.shape
    heads = parts // 3
    width = grad_all.shape[1]
    part = heads * HD
    return pl.pallas_call(
        attend_back_kernel,
        grid=(1,),
        in_specs=[whole(parts, LEN, HD), whole(LEN, width), whole(part, width)]
        + [pl.BlockSpec(memory_space=pl.ANY)] * (1 + len(first)),
        out_specs=whole(LEN, 3 * part),
        out_shape=jax.ShapeDtypeStruct((count, 3 * part), BF),
        scratch_shapes=[
            pltpu.VMEM((heads, LEN, HD), BF),
            pltpu.VMEM((LEN, 2 * part), F32),
            pltpu.VMEM((LEN, HD), F32),
            pltpu.VMEM((LEN, HD), F32),
            pltpu.VMEM((3, LEN, 128), F32),
            pltpu.SemaphoreType.DMA,
        ],
        compiler_params=pltpu.CompilerParams(vmem_limit_bytes=40 * MIB),
        cost_estimate=pl.CostEstimate(
            flops=20 * count * LEN * HD * heads, bytes_accessed=8 * MIB, transcendentals=count * LEN * heads
        ),
        name="attend_back",
    )(qkv, grad_all, wout, tables, *first)


def mlp_back_kernel(grad_ref, slope_ref, wdown_ref, pre_ref, pre_sum_ref, grad_sum_ref):
    grad = grad_ref[...]
    pre = (dot(grad, wdown_ref[...], 1, 1) * slope_ref[...]).astype(BF)
    pre_ref[...] = pre
    pre_sum = jnp.sum(pre.astype(F32), axis=0, keepdims=True)
    grad_sum = jnp.sum(grad.astype(F32), axis=0, keepdims=True)

    @pl.when(pl.program_id(0) == 0)
    def _():
        pre_sum_ref[...] = pre_sum
        grad_sum_ref[...] = grad_sum

    @pl.when(pl.program_id(0) > 0)
    def _():
        pre_sum_ref[...] += pre_sum
        grad_sum_ref[...] += grad_sum


def mlp_back(grad_all, slope, wdown):
    count, width = grad_all.shape
    ff = wdown.shape[0]
    rows = lambda w: pl.BlockSpec((ROWS, w), lambda g: (g, 0))
    return pl.pallas_call(
        mlp_back_kernel,
        grid=(count // ROWS,),
        in_specs=[rows(width), rows(ff), whole(ff, width)],
        out_specs=[rows(ff), whole(1, ff), whole(1, width)],
        out_shape=[
            jax.ShapeDtypeStruct((count, ff), BF), jax.ShapeDtypeStruct((1, ff), F32),
            jax.ShapeDtypeStruct((1, width), F32),
        ],
        compiler_params=pltpu.CompilerParams(vmem_limit_bytes=24 * MIB),
        cost_estimate=pl.CostEstimate(flops=2 * count * width * ff, bytes_accessed=8 * MIB, transcendentals=0),
        name="mlp_back",
    )(grad_all, slope, wdown)


def inputs_back_kernel(
    is_raw, slots, split, which_ref, projected_ref, pre_ref, x_ref, wqkv_ref, win_ref, gain_ref, *refs
):
    out_refs, sum_ref = refs[:-1], refs[-1]
    out_refs = out_refs[-slots:] if split else out_refs[-1:]
    step = pl.program_id(0)
    x = x_ref[...].astype(F32)
    n = normalize(x)[0] if is_raw else x
    first = dot(projected_ref[...], wqkv_ref[...], 1, 0)
    second = dot(pre_ref[...], win_ref[...], 1, 1)
    h = (first * gain_ref[0:1] + second * gain_ref[1:2]).astype(BF)
    column = lambda v: jnp.sum(v, axis=0, keepdims=True)
    sums = jnp.concatenate([column(first * n), column(second * n), column(first), column(second)], axis=0)

    @pl.when(step == 0)
    def _():
        sum_ref[...] = sums

    @pl.when(step > 0)
    def _():
        sum_ref[...] += sums

    if not split:
        out_refs[0][...] = h
        return
    for k in range(slots):

        @pl.when(step == k)
        def _(k=k):
            out_refs[k][...] = h


def inputs_back(which, split, is_raw, projected, pre, x, wqkv, win, gains, *first):
    slots = which.shape[0]
    qkv_width, width = wqkv.shape
    count, ff = x.shape[0], win.shape[1]
    rows = lambda w: pl.BlockSpec((ROWS, w), lambda g, ref: (ref[g], 0))
    outs = [whole(ROWS, width)] * slots if split else [rows(width)]
    shapes = [(ROWS, width)] * slots if split else [(count, width)]
    return pl.pallas_call(
        functools.partial(inputs_back_kernel, is_raw, slots, split),
        grid_spec=pltpu.PrefetchScalarGridSpec(
            num_scalar_prefetch=1,
            grid=(slots,),
            in_specs=[rows(qkv_width), rows(ff), rows(width)]
            + [whole(qkv_width, width), whole(width, ff), whole(2, width)]
            + [pl.BlockSpec(memory_space=pl.ANY)] * len(first),
            out_specs=outs + [whole(4, width)],
        ),
        out_shape=[jax.ShapeDtypeStruct(x, BF) for x in shapes] + [jax.ShapeDtypeStruct((4, width), F32)],
        compiler_params=pltpu.CompilerParams(vmem_limit_bytes=24 * MIB),
        cost_estimate=pl.CostEstimate(
            flops=2 * slots * ROWS * width * (qkv_width + ff), bytes_accessed=4 * MIB, transcendentals=0
        ),
        name="inputs_back",
    )(which, projected, pre, x, wqkv, win, gains, *first)


def place_kernel(layers, side_ref, *refs):
    out_qkv, out_out, out_in, out_down = refs[-4:]
    first = side_ref[0] == 0

    def both(l, low_a, low_b, high_a, high_b):
        half, qkv = low_b.shape[0], out_qkv.shape[1]
        out_in[l] = low_a[...].astype(F32)
        out_down[l] = high_a[...].astype(F32)
        out_qkv[l, 0:half] = low_b[...].astype(F32)
        out_qkv[l, half:qkv] = high_b[0 : qkv - half].astype(F32)
        out_out[l] = high_b[qkv - half : half].astype(F32)

    for l in range(layers):
        own, got = refs[4 * l : 4 * l + 2], refs[4 * l + 2 : 4 * l + 4]

        @pl.when(first)
        def _(l=l, own=own, got=got):
            both(l, *own, *got)

        @pl.when(jnp.logical_not(first))
        def _(l=l, own=own, got=got):
            both(l, *got, *own)


def place(side, sums, sizes):
    rows = (sizes[2], (sizes[0] + sizes[1]) // 2)
    layers = len(sums)
    arrays, specs = [], []
    tile = 128
    for pair in sums:
        for half in pair:
            for k, array in enumerate(half):
                at = 0 if k == 0 or array.shape[0] == rows[1] else rows[0] // rows[1]
                arrays.append(array)
                specs.append(pl.BlockSpec((rows[k], tile), lambda c, ref, at=at: (at, c)))
    width = arrays[0].shape[1]
    return pl.pallas_call(
        functools.partial(place_kernel, layers),
        grid_spec=pltpu.PrefetchScalarGridSpec(
            num_scalar_prefetch=1,
            grid=(width // tile,),
            in_specs=specs,
            out_specs=[pl.BlockSpec((layers, r, tile), lambda c, ref: (0, 0, c)) for r in sizes],
        ),
        out_shape=[jax.ShapeDtypeStruct((layers, r, width), F32) for r in sizes],
        compiler_params=pltpu.CompilerParams(vmem_limit_bytes=24 * MIB),
        cost_estimate=pl.CostEstimate(flops=0, bytes_accessed=20 * MIB, transcendentals=0),
        name="place",
    )(side.reshape(1), *arrays)


def after_kernel(count, *refs):
    for k in range(count):
        refs[len(refs) - count + k][...] = refs[k][...]


def after(arrays, *first):
    here = pl.BlockSpec(memory_space=pltpu.VMEM)
    return pl.pallas_call(
        functools.partial(after_kernel, len(arrays)),
        in_specs=[here] * len(arrays) + [pl.BlockSpec(memory_space=pl.ANY)] * len(first),
        out_specs=[here] * len(arrays),
        out_shape=[jax.ShapeDtypeStruct(x.shape, x.dtype) for x in arrays],
        cost_estimate=pl.CostEstimate(flops=0, bytes_accessed=MIB, transcendentals=0),
        compiler_params=pltpu.CompilerParams(vmem_limit_bytes=8 * MIB),
        name="after",
    )(*arrays, *first)


UP = [(0, 1), (1, 2), (2, 3)]
DOWN = [(1, 0), (2, 1), (3, 2)]


def send(x, pairs):
    return lax.ppermute(x, "tensor", pairs)


ENDS = [(0, 3), (3, 0)]


def gather_near(x):
    return send(x, UP), send(x, DOWN)


def gather_rest(x, near):
    below, above = near
    far = send(x, ENDS)
    a = send(above, [(1, 0), (2, 1)])
    c = send(below, [(2, 3), (1, 2)])
    i = lax.axis_index("tensor")
    pick = lambda *four: lax.select_n(jnp.broadcast_to(i, x.shape), *four)
    return jnp.concatenate(
        [pick(x, below, c, far), pick(above, x, below, c), pick(a, above, x, below), pick(far, a, above, x)], axis=0
    )


def gather_rows(x):
    return gather_rest(x, gather_near(x))


def whole_rows(x):
    return lax.all_gather(x, "tensor", axis=0, tiled=True)


def own_sum(x):
    return lax.psum_scatter(x, "tensor", scatter_dimension=0, tiled=True).astype(F32)


def partner(x, axis, bit):
    return lax.ppermute(x, axis, [(k, k ^ bit) for k in range(lax.axis_size(axis))])


def halve(x, bit):
    side = (lax.axis_index("dp") // bit) % 2
    half = x.shape[0] // 2
    mine = lax.dynamic_slice_in_dim(x, side * half, half, 0)
    other = lax.dynamic_slice_in_dim(x, (1 - side) * half, half, 0)
    return (mine.astype(F32) + partner(other, "dp", bit).astype(F32)).astype(BF), other


def plane_sum(y):
    size = lax.axis_size("dp")
    rows = y.shape[0] // 4
    k = (lax.axis_index("dp") // 2) % 4
    quarter = lambda j: lax.dynamic_slice_in_dim(y, (k ^ j) * rows, rows, 0)
    got = [partner(quarter(j), "dp", 2 * j) for j in (1, 2, 3)]
    own = sum(t.astype(F32) for t in [quarter(0)] + got).astype(BF)
    if size > 8:
        groups = [[g * 8 + k for g in range(size // 8)] for k in range(8)]
        own = lax.psum(own, "dp", axis_index_groups=groups)
    return own


def plane_gather(own):
    k = (lax.axis_index("dp") // 2) % 4
    four = [own] + [partner(own, "dp", 2 * j) for j in (1, 2, 3)]
    return jnp.concatenate([lax.select_n(jnp.broadcast_to(k ^ j, own.shape), *four) for j in range(4)], axis=0)


def sum_small(x, axis):
    size = lax.axis_size(axis)
    if size & (size - 1):
        return lax.psum(x, axis)
    bit = 1
    while bit < size:
        x = x + partner(x, axis, bit)
        bit *= 2
    return x


def body(tokens, cotangent, norm_gain, norm_shift, w_qkv, b_qkv, w_out, b_out, w_in, b_in, w_down, b_down):
    layers = w_qkv.shape[0]
    width = tokens.shape[1]
    wqkv = w_qkv.transpose(0, 2, 3, 1).reshape(layers, -1, width)
    sizes = (wqkv.shape[1], w_out.shape[1], width, w_down.shape[1])
    i = lax.axis_index("tensor")
    in_order = jnp.arange(4, dtype=jnp.int32)
    far_blocks = jnp.stack([(i + 2) % 4, 3 - i])
    near_blocks = jnp.stack([i ^ 1, i])
    tables = rope_tables()

    stream = tokens.astype(F32)
    gathered = gather_rows(tokens)
    grad_all = whole_rows(cotangent)
    kept = []
    for l in range(layers):
        last = l == layers - 1
        n_own, scale = normalize(stream)
        if l > 0:
            gathered = whole_rows(n_own.astype(BF))
        attn_in, mlp_in, qkv, hidden, slope = project(
            gathered, l == 0, norm_gain[l], norm_shift[l], tables, wqkv[l], b_qkv[l], w_in[l], b_in[l]
        )
        branch, mixed = attend(in_order, qkv, hidden, w_out[l], w_down[l])
        kept.append((n_own, scale, gathered, attn_in, mlp_in, qkv, hidden, slope, mixed))
        if not last:
            stream = stream + own_sum(branch) + b_out[l] + b_down[l]

    grad_stream = cotangent.astype(F32)
    biases, norms, sums = [None] * layers, [None] * layers, [None] * layers
    side = lax.axis_index("dp") % 2
    wait_gather, wait_attend, wait_inputs = (), (), ()
    for l in reversed(range(layers)):
        n_own, scale, gathered, attn_in, mlp_in, qkv, hidden, slope, mixed = kept[l]
        final = l == 0
        if l < layers - 1:
            grad_all = whole_rows(after([grad_stream.astype(BF)], *wait_gather)[0])
        if l == max(layers - 2, 0):
            late = own_sum(after([branch], grad_all)[0])
        grad_pre, pre_sum, grad_sum = mlp_back(grad_all, slope, w_down[l])
        mlp = [dot(mlp_in, grad_pre, 0, 0).astype(BF), dot(hidden, grad_all, 0, 0).astype(BF)]
        if final:
            mlp_half, mlp_sent = halve(jnp.concatenate(mlp, axis=0), 1)
            wait_attend += (mlp_sent,)
            wait_inputs += (mlp_half,)
        grad_projected = attend_back(qkv, grad_all, w_out[l], tables, mixed, *wait_attend)
        h, norms[l] = inputs_back(
            in_order, False, final, grad_projected, grad_pre, gathered, wqkv[l], w_in[l], norm_gain[l], *wait_inputs
        )
        h_own = own_sum(h)
        attention = jnp.concatenate(
            [dot(grad_projected, attn_in, 0, 0).astype(BF), dot(mixed, grad_all, 0, 0).astype(BF)], axis=0
        )
        biases[l] = (jnp.sum(grad_projected.astype(F32), 0), pre_sum[0], grad_sum[0])
        if final:
            attention_half, _ = halve(attention, 1)
            halves = [plane_gather(plane_sum(mlp_half)), plane_gather(plane_sum(attention_half))]
            sums[l] = (halves, [partner(x, "dp", 1) for x in halves])
            norms[l] = after([norms[l]], attention_half)[0]
        else:
            cut = attention.shape[0] // 2
            half, _ = halve(jnp.concatenate([mlp[0], attention[:cut], mlp[1], attention[cut:]], axis=0), 1)
            wait_gather = (half,)
            own = plane_sum(half)
            wait_attend = (own,)
            half = plane_gather(own)
            wait_inputs = (half,)
            got = partner(half, "dp", 1)
            sums[l] = ((half, half), (got, got))
        grad_stream = grad_stream + scale * (
            h_own
            - jnp.mean(h_own, axis=-1, keepdims=True)
            - n_own * jnp.mean(h_own * n_own, axis=-1, keepdims=True)
        )

    result = stream + late + b_out[layers - 1] + b_down[layers - 1]
    norm_sums = sum_small(jnp.concatenate(norms, axis=0), "tensor")
    flat = [norm_sums.reshape(-1)] + [v for three in biases for v in three]
    lengths = [v.shape[0] for v in flat]
    small = sum_small(jnp.concatenate(flat).reshape(-1, 128), "dp").reshape(-1)
    pieces = jnp.split(small, [sum(lengths[: k + 1]) for k in range(len(lengths) - 1)])
    norm_sums = pieces[0].reshape(layers, 4, width)
    g_qkv, g_out, g_in, g_down = place(side, sums, sizes)
    part = wqkv.shape[1] // 3
    g_qkv = g_qkv.reshape(layers, 3, part, width).transpose(0, 3, 1, 2)
    gb_qkv = jnp.stack([pieces[1 + 3 * l] for l in range(layers)]).reshape(layers, 3, part)
    gb_in = jnp.stack([pieces[2 + 3 * l] for l in range(layers)])
    gb_out = jnp.stack([pieces[3 + 3 * l] for l in range(layers)])
    return (
        result, grad_stream, norm_sums[:, 0:2], norm_sums[:, 2:4],
        g_qkv, gb_qkv, g_out, gb_out, g_in, gb_in, g_down, gb_out,
    )


def solution(mesh):
    rows = P(("dp", "tensor"), None)
    specs = (
        P(None, None, None, "tensor"), P(None, None, "tensor"), P(None, "tensor", None), P(),
        P(None, None, "tensor"), P(None, "tensor"), P(None, "tensor", None), P(),
    )
    both = (rows, rows, P(), P()) + specs
    return jax.shard_map(body, mesh=mesh, in_specs=both, out_specs=both, check_vma=False)
```

```python
import functools
import math

import jax
import jax.numpy as jnp
from jax import lax
from jax.experimental import pallas as pl
from jax.experimental.pallas import tpu as pltpu
from jax.sharding import PartitionSpec as P

HD = 64
ROT = 16
LEN = 1024
EPS = 1e-05
BF = jnp.bfloat16
F32 = jnp.float32
NEG = -1e30
ROWS = 256
MIB = 1024 * 1024


def dot(a, b, ca, cb):
    return lax.dot_general(a, b, (((ca,), (cb,)), ((), ())), preferred_element_type=F32)


def normalize(rows):
    centre = rows - jnp.mean(rows, axis=-1, keepdims=True)
    scale = lax.rsqrt(jnp.mean(centre * centre, axis=-1, keepdims=True) + EPS)
    return centre * scale, scale


def rope_tables():
    half = ROT // 2
    lane = jnp.arange(128, dtype=jnp.int32) % HD
    places = jnp.arange(LEN, dtype=jnp.int32).astype(F32)
    freqs = jnp.exp((lane % half).astype(F32) * (-2.0 * math.log(10000.0) / ROT))
    angles = places[:, None] * freqs[None, :]
    cosine = jnp.where(lane < ROT, jnp.cos(angles), 1.0)
    sine = jnp.sin(angles)
    left = jnp.where(lane < half, -sine, 0.0)
    right = jnp.where((lane >= half) & (lane < ROT), sine, 0.0)
    return jnp.stack([cosine, left, right])


def turn(group, tables, sign):
    swung = pltpu.roll(group, 128 - ROT // 2, 1) * tables[1] + pltpu.roll(group, ROT // 2, 1) * tables[2]
    return group * tables[0] + swung if sign > 0 else group * tables[0] - swung


def project_kernel(
    is_raw, x_ref, gain_ref, shift_ref, table_ref, wqkv_ref, bqkv_ref, win_ref, bin_ref,
    attn_ref, mlp_ref, qkv_ref, hidden_ref, slope_ref,
):
    x = x_ref[...].astype(F32)
    n = normalize(x)[0] if is_raw else x
    attn_in = (n * gain_ref[0:1] + shift_ref[0:1]).astype(BF)
    mlp_in = (n * gain_ref[1:2] + shift_ref[1:2]).astype(BF)
    attn_ref[...] = attn_in
    mlp_ref[...] = mlp_in
    projected = dot(attn_in, wqkv_ref[...], 1, 1) + bqkv_ref[...]
    part = projected.shape[1] // 3
    heads = part // HD
    tables = table_ref[...]
    pieces = []
    for g in range(2 * part // 128):
        pieces.append(turn(projected[:, g * 128 : (g + 1) * 128], tables, 1).astype(BF))
    rotated = jnp.concatenate(pieces, axis=1)
    for i in range(2 * heads):
        qkv_ref[i] = rotated[:, i * HD : (i + 1) * HD]
    value = projected[:, 2 * part :].astype(BF)
    for i in range(heads):
        qkv_ref[2 * heads + i] = value[:, i * HD : (i + 1) * HD]
    pre = dot(mlp_in, win_ref[...], 1, 0) + bin_ref[...]
    phi = 0.5 * (1.0 + lax.erf(pre * (1.0 / math.sqrt(2.0))))
    hidden_ref[...] = (pre * phi).astype(BF)
    slope_ref[...] = phi + pre * jnp.exp(-0.5 * pre * pre) * (1.0 / math.sqrt(2.0 * math.pi))


def whole(*shape):
    return pl.BlockSpec(shape, lambda *g: (0,) * len(shape))


def project(x, is_raw, gains, shifts, tables, wqkv, bqkv, win, bin_):
    count, width = x.shape
    qkv_width, ff = wqkv.shape[0], win.shape[1]
    parts = qkv_width // HD
    rows = lambda w: pl.BlockSpec((ROWS, w), lambda i: (i, 0))
    return pl.pallas_call(
        functools.partial(project_kernel, is_raw),
        grid=(count // ROWS,),
        in_specs=[rows(width), whole(2, width), whole(2, width), pl.BlockSpec((3, ROWS, 128), lambda i: (0, i, 0))]
        + [whole(qkv_width, width), whole(1, qkv_width), whole(width, ff), whole(1, ff)],
        out_specs=[
            rows(width), rows(width),
            pl.BlockSpec((parts, ROWS, HD), lambda i: (0, i, 0)),
            rows(ff), rows(ff),
        ],
        out_shape=[
            jax.ShapeDtypeStruct((count, width), BF),
            jax.ShapeDtypeStruct((count, width), BF),
            jax.ShapeDtypeStruct((parts, count, HD), BF),
            jax.ShapeDtypeStruct((count, ff), BF),
            jax.ShapeDtypeStruct((count, ff), F32),
        ],
        compiler_params=pltpu.CompilerParams(vmem_limit_bytes=32 * MIB),
        cost_estimate=pl.CostEstimate(
            flops=2 * count * width * (qkv_width + ff), bytes_accessed=12 * MIB, transcendentals=2 * count * ff
        ),
        name="project",
    )(x, gains, shifts, tables, wqkv, bqkv.reshape(1, -1), win, bin_.reshape(1, -1))


def attend_kernel(which_ref, qkv_ref, hidden_ref, wout_ref, wdown_ref, out_ref, mixed_ref):
    heads = qkv_ref.shape[0] // 3
    step = pl.program_id(0)
    block = which_ref[step]
    row = lax.broadcasted_iota(jnp.int32, (ROWS, ROWS), 0)
    col = lax.broadcasted_iota(jnp.int32, (ROWS, ROWS), 1)
    allowed = col <= row
    for b in range(LEN // ROWS):

        @pl.when(block == b)
        def _(b=b):
            lo, hi = b * ROWS, (b + 1) * ROWS
            for h in range(heads):
                q = (qkv_ref[h, lo:hi].astype(F32) * HD ** (-0.5)).astype(BF)
                s = dot(q, qkv_ref[heads + h, 0:hi], 1, 1)
                edge = jnp.where(allowed, s[:, lo:hi], NEG)
                s = edge if b == 0 else jnp.concatenate([s[:, :lo], edge], axis=1)
                e = jnp.exp(s - jnp.max(s, axis=1, keepdims=True))
                p = (e * (1.0 / jnp.sum(e, axis=1, keepdims=True))).astype(BF)
                o = dot(p, qkv_ref[2 * heads + h, 0:hi], 1, 0)
                mixed_ref[:, h * HD : (h + 1) * HD] = o.astype(BF)

    branch = dot(mixed_ref[...], wout_ref[...], 1, 0) + dot(hidden_ref[...], wdown_ref[...], 1, 0)
    out_ref[...] = branch.astype(BF)


def attend(which, qkv, hidden, wout, wdown):
    parts, count, _ = qkv.shape
    slots = which.shape[0]
    part, width = wout.shape
    ff = wdown.shape[0]
    rows = lambda w: pl.BlockSpec((ROWS, w), lambda g, ref: (ref[g], 0))
    return pl.pallas_call(
        attend_kernel,
        grid_spec=pltpu.PrefetchScalarGridSpec(
            num_scalar_prefetch=1,
            grid=(slots,),
            in_specs=[whole(parts, count, HD), rows(ff), whole(part, width), whole(ff, width)],
            out_specs=[rows(width), rows(part)],
        ),
        out_shape=[jax.ShapeDtypeStruct((count, width), BF), jax.ShapeDtypeStruct((count, part), BF)],
        compiler_params=pltpu.CompilerParams(vmem_limit_bytes=32 * MIB),
        cost_estimate=pl.CostEstimate(
            flops=8 * slots * ROWS * LEN * part, bytes_accessed=4 * MIB, transcendentals=slots * ROWS * LEN * parts // 3
        ),
        name="attend",
    )(which, qkv, hidden, wout, wdown)


def attend_back_kernel(qkv_ref, grad_ref, wout_ref, table_hbm, *refs):
    out_ref, sum_ref, gm_ref, dq_ref, dk_ref, dv_ref, table_ref, sem = refs[-8:]
    heads = qkv_ref.shape[0] // 3
    part = heads * HD
    fetch = pltpu.make_async_copy(table_hbm, table_ref, sem)
    fetch.start()
    for b in range(LEN // ROWS):
        lo, hi = b * ROWS, (b + 1) * ROWS
        gm = dot(grad_ref[lo:hi], wout_ref[...], 1, 1).astype(BF)
        for h in range(heads):
            gm_ref[h, lo:hi] = gm[:, h * HD : (h + 1) * HD]
    row = lax.broadcasted_iota(jnp.int32, (ROWS, ROWS), 0)
    col = lax.broadcasted_iota(jnp.int32, (ROWS, ROWS), 1)
    allowed = row <= col
    scale = HD ** (-0.5)
    blocks = LEN // ROWS
    for h in range(heads):
        for b in reversed(range(blocks)):
            lo, hi = b * ROWS, (b + 1) * ROWS
            q = (qkv_ref[h, lo:hi].astype(F32) * scale).astype(BF)
            key = qkv_ref[heads + h, 0:hi]
            s = dot(key, q, 1, 1)
            edge = jnp.where(allowed, s[lo:hi], NEG)
            s = edge if b == 0 else jnp.concatenate([s[:lo], edge], axis=0)
            e = jnp.exp(s - jnp.max(s, axis=0, keepdims=True))
            p = e * (1.0 / jnp.sum(e, axis=0, keepdims=True))
            gm = gm_ref[h, lo:hi]
            dv = dot(p.astype(BF), gm, 1, 0)
            dp = dot(qkv_ref[2 * heads + h, 0:hi], gm, 1, 1)
            delta = jnp.sum(p * dp, axis=0, keepdims=True)
            ds = (p * (dp - delta)).astype(BF)
            dk = dot(ds, q, 1, 0)
            dq = dot(ds, key, 0, 0) * scale
            dq_ref[lo:hi, h * HD : (h + 1) * HD] = dq
            if b == blocks - 1:
                dk_ref[...] = dk
                dv_ref[...] = dv
            else:
                dk_ref[0:hi] += dk
                dv_ref[0:hi] += dv
        dq_ref[:, part + h * HD : part + (h + 1) * HD] = dk_ref[...]
        value = dv_ref[...].astype(BF)
        lanes = slice(2 * part + h * HD, 2 * part + (h + 1) * HD)
        out_ref[:, lanes] = value
        sum_ref[:, lanes] = jnp.sum(value.astype(F32), axis=0, keepdims=True)
    fetch.wait()
    tables = table_ref[...]
    for g in range(2 * part // 128):
        lanes = slice(g * 128, (g + 1) * 128)
        value = turn(dq_ref[:, lanes], tables, -1).astype(BF)
        out_ref[:, lanes] = value
        sum_ref[:, lanes] = jnp.sum(value.astype(F32), axis=0, keepdims=True)


def attend_back(qkv, grad_all, wout, tables, *first):
    parts, count, _ = qkv.shape
    heads = parts // 3
    width = grad_all.shape[1]
    part = heads * HD
    return pl.pallas_call(
        attend_back_kernel,
        grid=(1,),
        in_specs=[whole(parts, LEN, HD), whole(LEN, width), whole(part, width)]
        + [pl.BlockSpec(memory_space=pl.ANY)] * (1 + len(first)),
        out_specs=[whole(LEN, 3 * part), whole(1, 3 * part)],
        out_shape=[jax.ShapeDtypeStruct((count, 3 * part), BF), jax.ShapeDtypeStruct((1, 3 * part), F32)],
        scratch_shapes=[
            pltpu.VMEM((heads, LEN, HD), BF),
            pltpu.VMEM((LEN, 2 * part), F32),
            pltpu.VMEM((LEN, HD), F32),
            pltpu.VMEM((LEN, HD), F32),
            pltpu.VMEM((3, LEN, 128), F32),
            pltpu.SemaphoreType.DMA,
        ],
        compiler_params=pltpu.CompilerParams(vmem_limit_bytes=40 * MIB),
        cost_estimate=pl.CostEstimate(
            flops=20 * count * LEN * HD * heads, bytes_accessed=8 * MIB, transcendentals=count * LEN * heads
        ),
        name="attend_back",
    )(qkv, grad_all, wout, tables, *first)


def mlp_back_kernel(grad_ref, slope_ref, wdown_ref, pre_ref, pre_sum_ref, grad_sum_ref):
    grad = grad_ref[...]
    pre = (dot(grad, wdown_ref[...], 1, 1) * slope_ref[...]).astype(BF)
    pre_ref[...] = pre
    pre_sum = jnp.sum(pre.astype(F32), axis=0, keepdims=True)
    grad_sum = jnp.sum(grad.astype(F32), axis=0, keepdims=True)

    @pl.when(pl.program_id(0) == 0)
    def _():
        pre_sum_ref[...] = pre_sum
        grad_sum_ref[...] = grad_sum

    @pl.when(pl.program_id(0) > 0)
    def _():
        pre_sum_ref[...] += pre_sum
        grad_sum_ref[...] += grad_sum


def mlp_back(grad_all, slope, wdown):
    count, width = grad_all.shape
    ff = wdown.shape[0]
    rows = lambda w: pl.BlockSpec((ROWS, w), lambda g: (g, 0))
    return pl.pallas_call(
        mlp_back_kernel,
        grid=(count // ROWS,),
        in_specs=[rows(width), rows(ff), whole(ff, width)],
        out_specs=[rows(ff), whole(1, ff), whole(1, width)],
        out_shape=[
            jax.ShapeDtypeStruct((count, ff), BF), jax.ShapeDtypeStruct((1, ff), F32),
            jax.ShapeDtypeStruct((1, width), F32),
        ],
        compiler_params=pltpu.CompilerParams(vmem_limit_bytes=24 * MIB),
        cost_estimate=pl.CostEstimate(flops=2 * count * width * ff, bytes_accessed=8 * MIB, transcendentals=0),
        name="mlp_back",
    )(grad_all, slope, wdown)


def inputs_back_kernel(
    is_raw, slots, split, which_ref, projected_ref, pre_ref, x_ref, wqkv_ref, win_ref, gain_ref, *refs
):
    out_refs, sum_ref = refs[:-1], refs[-1]
    out_refs = out_refs[-slots:] if split else out_refs[-1:]
    step = pl.program_id(0)
    x = x_ref[...].astype(F32)
    n = normalize(x)[0] if is_raw else x
    first = dot(projected_ref[...], wqkv_ref[...], 1, 0)
    second = dot(pre_ref[...], win_ref[...], 1, 1)
    h = (first * gain_ref[0:1] + second * gain_ref[1:2]).astype(BF)
    column = lambda v: jnp.sum(v, axis=0, keepdims=True)
    sums = jnp.concatenate([column(first * n), column(second * n), column(first), column(second)], axis=0)

    @pl.when(step == 0)
    def _():
        sum_ref[...] = sums

    @pl.when(step > 0)
    def _():
        sum_ref[...] += sums

    if not split:
        out_refs[0][...] = h
        return
    for k in range(slots):

        @pl.when(step == k)
        def _(k=k):
            out_refs[k][...] = h


def inputs_back(which, split, is_raw, projected, pre, x, wqkv, win, gains, *first):
    slots = which.shape[0]
    qkv_width, width = wqkv.shape
    count, ff = x.shape[0], win.shape[1]
    rows = lambda w: pl.BlockSpec((ROWS, w), lambda g, ref: (ref[g], 0))
    outs = [whole(ROWS, width)] * slots if split else [rows(width)]
    shapes = [(ROWS, width)] * slots if split else [(count, width)]
    return pl.pallas_call(
        functools.partial(inputs_back_kernel, is_raw, slots, split),
        grid_spec=pltpu.PrefetchScalarGridSpec(
            num_scalar_prefetch=1,
            grid=(slots,),
            in_specs=[rows(qkv_width), rows(ff), rows(width)]
            + [whole(qkv_width, width), whole(width, ff), whole(2, width)]
            + [pl.BlockSpec(memory_space=pl.ANY)] * len(first),
            out_specs=outs + [whole(4, width)],
        ),
        out_shape=[jax.ShapeDtypeStruct(x, BF) for x in shapes] + [jax.ShapeDtypeStruct((4, width), F32)],
        compiler_params=pltpu.CompilerParams(vmem_limit_bytes=24 * MIB),
        cost_estimate=pl.CostEstimate(
            flops=2 * slots * ROWS * width * (qkv_width + ff), bytes_accessed=4 * MIB, transcendentals=0
        ),
        name="inputs_back",
    )(which, projected, pre, x, wqkv, win, gains, *first)


def place_kernel(side_ref, own_a, own_b, got_a, got_b, *refs):
    out_qkv, out_out, out_in, out_down = refs[-4:]
    first = side_ref[0] == 0

    def both(low_a, low_b, high_a, high_b):
        half, qkv = low_b.shape[0], out_qkv.shape[1]
        out_in[0] = low_a[...].astype(F32)
        out_down[0] = high_a[...].astype(F32)
        out_qkv[0, 0:half] = low_b[...].astype(F32)
        out_qkv[0, half:qkv] = high_b[0 : qkv - half].astype(F32)
        out_out[0] = high_b[qkv - half : half].astype(F32)

    @pl.when(first)
    def _():
        both(own_a, own_b, got_a, got_b)

    @pl.when(jnp.logical_not(first))
    def _():
        both(got_a, got_b, own_a, own_b)


def place(layer, layers, side, own, got, sizes, earlier):
    rows = (sizes[2], (sizes[0] + sizes[1]) // 2)
    arrays, specs = [], []
    tile = 256
    for half in (own, got):
        for k, array in enumerate(half):
            at = 0 if k == 0 or array.shape[0] == rows[1] else rows[0] // rows[1]
            arrays.append(array)
            specs.append(pl.BlockSpec((rows[k], tile), lambda c, ref, at=at: (at, c)))
    width = arrays[0].shape[1]
    more = list(earlier)
    return pl.pallas_call(
        place_kernel,
        grid_spec=pltpu.PrefetchScalarGridSpec(
            num_scalar_prefetch=1,
            grid=(width // tile,),
            in_specs=specs + [pl.BlockSpec(memory_space=pl.ANY)] * len(more),
            out_specs=[pl.BlockSpec((1, r, tile), lambda c, ref: (layer, 0, c)) for r in sizes],
        ),
        out_shape=[jax.ShapeDtypeStruct((layers, r, width), F32) for r in sizes],
        input_output_aliases={5 + k: k for k in range(len(more))},
        compiler_params=pltpu.CompilerParams(vmem_limit_bytes=24 * MIB),
        cost_estimate=pl.CostEstimate(flops=0, bytes_accessed=10 * MIB, transcendentals=0),
        name="place",
    )(side.reshape(1), *arrays, *more)


def weights_kernel(mlp, attention, side_ref, *refs):
    own_ref, other_ref = refs[-2:]
    take = list(refs[: 4 * mlp + 4 * attention])
    low, high = [], []
    if mlp:
        mlp_in, pre, hidden, grad = take[:4]
        take = take[4:]
        for c in range(0, mlp_in.shape[1], ROWS):
            low.append(dot(mlp_in[:, c : c + ROWS], pre[...], 0, 0).astype(BF))
        for c in range(0, hidden.shape[1], ROWS):
            high.append(dot(hidden[:, c : c + ROWS], grad[...], 0, 0).astype(BF))
    if attention:
        projected, attn_in, mixed, grad = take
        cut = (projected.shape[1] + mixed.shape[1]) // 2
        low.append(dot(projected[:, :cut], attn_in[...], 0, 0).astype(BF))
        high.append(dot(projected[:, cut:], attn_in[...], 0, 0).astype(BF))
        high.append(dot(mixed[...], grad[...], 0, 0).astype(BF))

    def write(ref, pieces):
        at = 0
        for piece in pieces:
            ref[at : at + piece.shape[0]] = piece
            at += piece.shape[0]

    @pl.when(side_ref[0] == 0)
    def _():
        write(own_ref, low)
        write(other_ref, high)

    @pl.when(side_ref[0] != 0)
    def _():
        write(own_ref, high)
        write(other_ref, low)


def weights_back(side, mlp=(), attention=(), first=()):
    arrays = [*mlp, *attention]
    width = arrays[1].shape[1]
    rows = (mlp[0].shape[1] if mlp else 0) + ((attention[0].shape[1] + attention[2].shape[1]) // 2 if attention else 0)
    return pl.pallas_call(
        functools.partial(weights_kernel, bool(mlp), bool(attention)),
        in_specs=[pl.BlockSpec(memory_space=pltpu.SMEM)]
        + [pl.BlockSpec(memory_space=pltpu.VMEM)] * len(arrays)
        + [pl.BlockSpec(memory_space=pl.ANY)] * len(first),
        out_specs=[pl.BlockSpec(memory_space=pltpu.VMEM)] * 2,
        out_shape=[jax.ShapeDtypeStruct((rows, width), BF)] * 2,
        compiler_params=pltpu.CompilerParams(vmem_limit_bytes=16 * MIB),
        cost_estimate=pl.CostEstimate(
            flops=4 * rows * width * arrays[0].shape[0], bytes_accessed=6 * MIB, transcendentals=0
        ),
        name="weights_back",
    )(side.reshape(1), *arrays, *first)


def quarters_kernel(which_ref, own_ref, got_ref, *out_refs):
    step = pl.program_id(0)
    total = (own_ref[...].astype(F32) + got_ref[...].astype(F32)).astype(BF)
    for k in range(4):

        @pl.when(step == k)
        def _(k=k):
            out_refs[k][...] = total


def quarters(which, own, got):
    rows, width = own.shape[0] // 4, own.shape[1]
    spec = pl.BlockSpec((rows, width), lambda g, ref: (ref[g], 0))
    return pl.pallas_call(
        quarters_kernel,
        grid_spec=pltpu.PrefetchScalarGridSpec(
            num_scalar_prefetch=1,
            grid=(4,),
            in_specs=[spec, spec],
            out_specs=[whole(rows, width)] * 4,
        ),
        out_shape=[jax.ShapeDtypeStruct((rows, width), BF)] * 4,
        compiler_params=pltpu.CompilerParams(vmem_limit_bytes=16 * MIB),
        cost_estimate=pl.CostEstimate(flops=0, bytes_accessed=6 * MIB, transcendentals=0),
        name="quarters",
    )(which, own, got)


def forward_norm_kernel(x_ref, branch_ref, out_ref, down_ref, stream_ref, n_ref):
    stream = x_ref[...].astype(F32) + branch_ref[...].astype(F32) + out_ref[...] + down_ref[...]
    stream_ref[...] = stream
    n_ref[...] = normalize(stream)[0].astype(BF)


def forward_norm(x, branch, out_bias, down_bias):
    here = pl.BlockSpec(memory_space=pltpu.VMEM)
    return pl.pallas_call(
        forward_norm_kernel,
        in_specs=[here] * 4,
        out_specs=[here] * 2,
        out_shape=[jax.ShapeDtypeStruct(x.shape, F32), jax.ShapeDtypeStruct(x.shape, BF)],
        compiler_params=pltpu.CompilerParams(vmem_limit_bytes=12 * MIB),
        cost_estimate=pl.CostEstimate(flops=0, bytes_accessed=2 * MIB, transcendentals=0),
        name="forward_norm",
    )(x, branch, out_bias.reshape(1, -1), down_bias.reshape(1, -1))


def backward_norm_kernel(x_ref, h_ref, grad_ref, *refs):
    n, scale = normalize(x_ref[...].astype(F32))
    h = h_ref[...].astype(F32)
    mean = lambda v: jnp.mean(v, axis=-1, keepdims=True)
    grad = grad_ref[...].astype(F32) + scale * (h - mean(h) - n * mean(h * n))
    refs[-2][...] = grad
    refs[-1][...] = grad.astype(BF)


def backward_norm(x, h, grad, first=()):
    here = pl.BlockSpec(memory_space=pltpu.VMEM)
    return pl.pallas_call(
        backward_norm_kernel,
        in_specs=[here] * 3 + [pl.BlockSpec(memory_space=pl.ANY)] * len(first),
        out_specs=[here] * 2,
        out_shape=[jax.ShapeDtypeStruct(x.shape, F32), jax.ShapeDtypeStruct(x.shape, BF)],
        compiler_params=pltpu.CompilerParams(vmem_limit_bytes=12 * MIB),
        cost_estimate=pl.CostEstimate(flops=0, bytes_accessed=2 * MIB, transcendentals=0),
        name="backward_norm",
    )(x, h, grad, *first)


def after_kernel(count, *refs):
    for k in range(count):
        refs[len(refs) - count + k][...] = refs[k][...]


def after(arrays, *first):
    here = pl.BlockSpec(memory_space=pltpu.VMEM)
    return pl.pallas_call(
        functools.partial(after_kernel, len(arrays)),
        in_specs=[here] * len(arrays) + [pl.BlockSpec(memory_space=pl.ANY)] * len(first),
        out_specs=[here] * len(arrays),
        out_shape=[jax.ShapeDtypeStruct(x.shape, x.dtype) for x in arrays],
        cost_estimate=pl.CostEstimate(flops=0, bytes_accessed=MIB, transcendentals=0),
        compiler_params=pltpu.CompilerParams(vmem_limit_bytes=8 * MIB),
        name="after",
    )(*arrays, *first)


UP = [(0, 1), (1, 2), (2, 3)]
DOWN = [(1, 0), (2, 1), (3, 2)]


def send(x, pairs):
    return lax.ppermute(x, "tensor", pairs)


ENDS = [(0, 3), (3, 0)]


def gather_near(x):
    return send(x, UP), send(x, DOWN), send(x, ENDS)


def gather_rest(x, near):
    below, above, far = near
    a = send(above, [(1, 0), (2, 1)])
    c = send(below, [(2, 3), (1, 2)])
    i = lax.axis_index("tensor")
    pick = lambda *four: lax.select_n(jnp.broadcast_to(i, x.shape), *four)
    return jnp.concatenate(
        [pick(x, below, c, far), pick(above, x, below, c), pick(a, above, x, below), pick(far, a, above, x)], axis=0
    )


def gather_rows(x):
    return gather_rest(x, gather_near(x))


def whole_rows(x):
    return lax.all_gather(x, "tensor", axis=0, tiled=True)


def own_sum(x):
    return lax.psum_scatter(x, "tensor", scatter_dimension=0, tiled=True)


def partner(x, axis, bit):
    return lax.ppermute(x, axis, [(k, k ^ bit) for k in range(lax.axis_size(axis))])


def plane_send(own, other):
    k = (lax.axis_index("dp") // 2) % 4
    which = jnp.stack([k ^ j for j in range(4)])
    return quarters(which, own, partner(other, "dp", 1))


def plane_sum(four):
    size = lax.axis_size("dp")
    got = [partner(four[j], "dp", 2 * j) for j in (1, 2, 3)]
    own = sum(t.astype(F32) for t in [four[0]] + got).astype(BF)
    if size > 8:
        groups = [[g * 8 + k for g in range(size // 8)] for k in range(8)]
        own = lax.psum(own, "dp", axis_index_groups=groups)
    return own


def plane_gather(own):
    k = (lax.axis_index("dp") // 2) % 4
    four = [own] + [partner(own, "dp", 2 * j) for j in (1, 2, 3)]
    return jnp.concatenate([lax.select_n(jnp.broadcast_to(k ^ j, own.shape), *four) for j in range(4)], axis=0)


def sum_small(x, axis):
    size = lax.axis_size(axis)
    if size & (size - 1):
        return lax.psum(x, axis)
    bit = 1
    while bit < size:
        x = x + partner(x, axis, bit)
        bit *= 2
    return x


def body(tokens, cotangent, norm_gain, norm_shift, w_qkv, b_qkv, w_out, b_out, w_in, b_in, w_down, b_down):
    layers = w_qkv.shape[0]
    width = tokens.shape[1]
    wqkv = w_qkv.transpose(0, 2, 3, 1).reshape(layers, -1, width)
    sizes = (wqkv.shape[1], w_out.shape[1], width, w_down.shape[1])
    i = lax.axis_index("tensor")
    in_order = jnp.arange(4, dtype=jnp.int32)
    far_blocks = jnp.stack([(i + 2) % 4, 3 - i])
    near_blocks = jnp.stack([i ^ 1, i])
    tables = rope_tables()

    stream = tokens
    gathered = gather_rows(tokens)
    grad_all = whole_rows(cotangent)
    kept = []
    for l in range(layers):
        last = l == layers - 1
        if l > 0:
            gathered = whole_rows(n_own)
        attn_in, mlp_in, qkv, hidden, slope = project(
            gathered, l == 0, norm_gain[l], norm_shift[l], tables, wqkv[l], b_qkv[l], w_in[l], b_in[l]
        )
        branch, mixed = attend(in_order, qkv, hidden, w_out[l], w_down[l])
        kept.append((stream, gathered, attn_in, mlp_in, qkv, hidden, slope, mixed))
        if not last:
            stream, n_own = forward_norm(stream, own_sum(branch), b_out[l], b_down[l])

    grad_stream = cotangent
    biases, norms = [None] * layers, [None] * layers
    side = lax.axis_index("dp") % 2
    placed = ()
    wait_gather, wait_near, wait_attend, wait_inputs = (), (), (), ()
    for l in reversed(range(layers)):
        stream_in, gathered, attn_in, mlp_in, qkv, hidden, slope, mixed = kept[l]
        final = l == 0
        if l < layers - 1:
            below, above, far = gather_near(grad_low)
            below, above = after([below, above], *wait_near)
            grad_all = gather_rest(grad_low, (below, above, far))
        if l == max(layers - 2, 0):
            late = own_sum(after([branch], grad_all)[0])
        grad_pre, pre_sum, grad_sum = mlp_back(grad_all, slope, w_down[l])
        mlp = (mlp_in, grad_pre, hidden, grad_all)
        if final:
            mlp_own, mlp_other = weights_back(side, mlp=mlp)
            wait_attend += (mlp_other,)
        grad_projected, projected_sum = attend_back(qkv, grad_all, w_out[l], tables, mixed, *wait_attend)
        if final:
            mlp_four = plane_send(mlp_own, mlp_other)
            wait_inputs += (mlp_four[1],)
        h, norms[l] = inputs_back(
            in_order, False, final, grad_projected, grad_pre, gathered, wqkv[l], w_in[l], norm_gain[l], *wait_inputs
        )
        h_own = own_sum(h)
        attention = (grad_projected, attn_in, mixed, grad_all)
        biases[l] = (projected_sum[0], pre_sum[0], grad_sum[0])
        if final:
            attention_own, attention_other = weights_back(side, attention=attention, first=(h,))
            attention_four = plane_send(attention_own, attention_other)
            own = [plane_gather(plane_sum(mlp_four)), plane_gather(plane_sum(attention_four))]
            got = [partner(x, "dp", 1) for x in own]
            norms[l] = after([norms[l]], attention_other, placed[1])[0]
            placed = place(l, layers, side, own, got, sizes, placed)
            wait_gather = ()
        else:
            own, other = weights_back(side, mlp=mlp, attention=attention, first=(h,))
            four = plane_send(own, other)
            wait_gather = (four[1],)
            own = plane_sum(four)
            wait_near = (own,)
            own = plane_gather(own)
            wait_attend = (own,)
            got = partner(own, "dp", 1)
            placed = place(l, layers, side, (own, own), (got, got), sizes, placed)
        grad_stream, grad_low = backward_norm(stream_in, h_own, grad_stream, wait_gather)

    result = stream + late.astype(F32) + b_out[layers - 1] + b_down[layers - 1]
    norm_sums = sum_small(jnp.concatenate(norms, axis=0), "tensor")
    part = wqkv.shape[1]
    pad = lambda v: jnp.pad(v, (0, width - v.shape[0]))[None]
    small = sum_small(jnp.concatenate([norm_sums] + [pad(v) for three in biases for v in three], axis=0), "dp")
    norm_sums = small[: 4 * layers].reshape(layers, 4, width)
    rest = small[4 * layers :].reshape(layers, 3, width)
    g_qkv, g_out, g_in, g_down = placed
    g_qkv = g_qkv.reshape(layers, 3, part // 3, width).transpose(0, 3, 1, 2)
    gb_qkv = rest[:, 0, :part].reshape(layers, 3, part // 3)
    gb_in = rest[:, 1, : b_in.shape[1]]
    gb_out = rest[:, 2]
    return (
        result, grad_stream, norm_sums[:, 0:2], norm_sums[:, 2:4],
        g_qkv, gb_qkv, g_out, gb_out, g_in, gb_in, g_down, gb_out,
    )


def solution(mesh):
    rows = P(("dp", "tensor"), None)
    specs = (
        P(None, None, None, "tensor"), P(None, None, "tensor"), P(None, "tensor", None), P(),
        P(None, None, "tensor"), P(None, "tensor"), P(None, "tensor", None), P(),
    )
    both = (rows, rows, P(), P()) + specs
    return jax.shard_map(body, mesh=mesh, in_specs=both, out_specs=both, check_vma=False)
```

```python
import functools
import math

import jax
import jax.numpy as jnp
from jax import lax
from jax.experimental import pallas as pl
from jax.experimental.pallas import tpu as pltpu
from jax.sharding import PartitionSpec as P

HD = 64
ROT = 16
LEN = 1024
EPS = 1e-05
BF = jnp.bfloat16
F32 = jnp.float32
NEG = -1e30
ROWS = 256
MIB = 1024 * 1024


def dot(a, b, ca, cb):
    return lax.dot_general(a, b, (((ca,), (cb,)), ((), ())), preferred_element_type=F32)


def normalize(rows):
    centre = rows - jnp.mean(rows, axis=-1, keepdims=True)
    scale = lax.rsqrt(jnp.mean(centre * centre, axis=-1, keepdims=True) + EPS)
    return centre * scale, scale


def rope_tables():
    half = ROT // 2
    lane = jnp.arange(128, dtype=jnp.int32) % HD
    places = jnp.arange(LEN, dtype=jnp.int32).astype(F32)
    freqs = jnp.exp((lane % half).astype(F32) * (-2.0 * math.log(10000.0) / ROT))
    angles = places[:, None] * freqs[None, :]
    cosine = jnp.where(lane < ROT, jnp.cos(angles), 1.0)
    sine = jnp.sin(angles)
    left = jnp.where(lane < half, -sine, 0.0)
    right = jnp.where((lane >= half) & (lane < ROT), sine, 0.0)
    return jnp.stack([cosine, left, right])


def turn(group, tables, sign):
    swung = pltpu.roll(group, 128 - ROT // 2, 1) * tables[1] + pltpu.roll(group, ROT // 2, 1) * tables[2]
    return group * tables[0] + swung if sign > 0 else group * tables[0] - swung


def project_kernel(
    is_raw, x_ref, gain_ref, shift_ref, table_ref, wqkv_ref, bqkv_ref, win_ref, bin_ref,
    attn_ref, mlp_ref, qkv_ref, hidden_ref, slope_ref,
):
    x = x_ref[...].astype(F32)
    n = normalize(x)[0] if is_raw else x
    attn_in = (n * gain_ref[0:1] + shift_ref[0:1]).astype(BF)
    mlp_in = (n * gain_ref[1:2] + shift_ref[1:2]).astype(BF)
    attn_ref[...] = attn_in
    mlp_ref[...] = mlp_in
    projected = dot(attn_in, wqkv_ref[...], 1, 1) + bqkv_ref[...]
    part = projected.shape[1] // 3
    heads = part // HD
    tables = table_ref[...]
    pieces = []
    for g in range(2 * part // 128):
        pieces.append(turn(projected[:, g * 128 : (g + 1) * 128], tables, 1).astype(BF))
    rotated = jnp.concatenate(pieces, axis=1)
    for i in range(2 * heads):
        qkv_ref[i] = rotated[:, i * HD : (i + 1) * HD]
    value = projected[:, 2 * part :].astype(BF)
    for i in range(heads):
        qkv_ref[2 * heads + i] = value[:, i * HD : (i + 1) * HD]
    pre = dot(mlp_in, win_ref[...], 1, 0) + bin_ref[...]
    phi = 0.5 * (1.0 + lax.erf(pre * (1.0 / math.sqrt(2.0))))
    hidden_ref[...] = (pre * phi).astype(BF)
    slope_ref[...] = phi + pre * jnp.exp(-0.5 * pre * pre) * (1.0 / math.sqrt(2.0 * math.pi))


def whole(*shape):
    return pl.BlockSpec(shape, lambda *g: (0,) * len(shape))


def project(x, is_raw, gains, shifts, tables, wqkv, bqkv, win, bin_):
    count, width = x.shape
    qkv_width, ff = wqkv.shape[0], win.shape[1]
    parts = qkv_width // HD
    rows = lambda w: pl.BlockSpec((ROWS, w), lambda i: (i, 0))
    return pl.pallas_call(
        functools.partial(project_kernel, is_raw),
        grid=(count // ROWS,),
        in_specs=[rows(width), whole(2, width), whole(2, width), pl.BlockSpec((3, ROWS, 128), lambda i: (0, i, 0))]
        + [whole(qkv_width, width), whole(1, qkv_width), whole(width, ff), whole(1, ff)],
        out_specs=[
            rows(width), rows(width),
            pl.BlockSpec((parts, ROWS, HD), lambda i: (0, i, 0)),
            rows(ff), rows(ff),
        ],
        out_shape=[
            jax.ShapeDtypeStruct((count, width), BF),
            jax.ShapeDtypeStruct((count, width), BF),
            jax.ShapeDtypeStruct((parts, count, HD), BF),
            jax.ShapeDtypeStruct((count, ff), BF),
            jax.ShapeDtypeStruct((count, ff), F32),
        ],
        compiler_params=pltpu.CompilerParams(vmem_limit_bytes=32 * MIB),
        cost_estimate=pl.CostEstimate(
            flops=2 * count * width * (qkv_width + ff), bytes_accessed=12 * MIB, transcendentals=2 * count * ff
        ),
        name="project",
    )(x, gains, shifts, tables, wqkv, bqkv.reshape(1, -1), win, bin_.reshape(1, -1))


def attend_kernel(which_ref, qkv_ref, hidden_ref, wout_ref, wdown_ref, out_ref, mixed_ref):
    heads = qkv_ref.shape[0] // 3
    step = pl.program_id(0)
    block = which_ref[step]
    row = lax.broadcasted_iota(jnp.int32, (ROWS, ROWS), 0)
    col = lax.broadcasted_iota(jnp.int32, (ROWS, ROWS), 1)
    allowed = col <= row
    for b in range(LEN // ROWS):

        @pl.when(block == b)
        def _(b=b):
            lo, hi = b * ROWS, (b + 1) * ROWS
            for h in range(heads):
                q = (qkv_ref[h, lo:hi].astype(F32) * HD ** (-0.5)).astype(BF)
                s = dot(q, qkv_ref[heads + h, 0:hi], 1, 1)
                edge = jnp.where(allowed, s[:, lo:hi], NEG)
                s = edge if b == 0 else jnp.concatenate([s[:, :lo], edge], axis=1)
                e = jnp.exp(s - jnp.max(s, axis=1, keepdims=True))
                p = (e * (1.0 / jnp.sum(e, axis=1, keepdims=True))).astype(BF)
                o = dot(p, qkv_ref[2 * heads + h, 0:hi], 1, 0)
                mixed_ref[:, h * HD : (h + 1) * HD] = o.astype(BF)

    branch = dot(mixed_ref[...], wout_ref[...], 1, 0) + dot(hidden_ref[...], wdown_ref[...], 1, 0)
    out_ref[...] = branch.astype(BF)


def attend(which, qkv, hidden, wout, wdown):
    parts, count, _ = qkv.shape
    slots = which.shape[0]
    part, width = wout.shape
    ff = wdown.shape[0]
    rows = lambda w: pl.BlockSpec((ROWS, w), lambda g, ref: (ref[g], 0))
    return pl.pallas_call(
        attend_kernel,
        grid_spec=pltpu.PrefetchScalarGridSpec(
            num_scalar_prefetch=1,
            grid=(slots,),
            in_specs=[whole(parts, count, HD), rows(ff), whole(part, width), whole(ff, width)],
            out_specs=[rows(width), rows(part)],
        ),
        out_shape=[jax.ShapeDtypeStruct((count, width), BF), jax.ShapeDtypeStruct((count, part), BF)],
        compiler_params=pltpu.CompilerParams(vmem_limit_bytes=32 * MIB),
        cost_estimate=pl.CostEstimate(
            flops=8 * slots * ROWS * LEN * part, bytes_accessed=4 * MIB, transcendentals=slots * ROWS * LEN * parts // 3
        ),
        name="attend",
    )(which, qkv, hidden, wout, wdown)


def attend_back_kernel(qkv_ref, grad_ref, wout_ref, table_hbm, *refs):
    out_ref, sum_ref, gm_ref, dq_ref, dk_ref, dv_ref, table_ref, sem = refs[-8:]
    heads = qkv_ref.shape[0] // 3
    part = heads * HD
    fetch = pltpu.make_async_copy(table_hbm, table_ref, sem)
    fetch.start()
    for b in range(LEN // ROWS):
        lo, hi = b * ROWS, (b + 1) * ROWS
        gm = dot(grad_ref[lo:hi], wout_ref[...], 1, 1).astype(BF)
        for h in range(heads):
            gm_ref[h, lo:hi] = gm[:, h * HD : (h + 1) * HD]
    row = lax.broadcasted_iota(jnp.int32, (ROWS, ROWS), 0)
    col = lax.broadcasted_iota(jnp.int32, (ROWS, ROWS), 1)
    allowed = row <= col
    scale = HD ** (-0.5)
    blocks = LEN // ROWS
    for h in range(heads):
        for b in reversed(range(blocks)):
            lo, hi = b * ROWS, (b + 1) * ROWS
            q = (qkv_ref[h, lo:hi].astype(F32) * scale).astype(BF)
            key = qkv_ref[heads + h, 0:hi]
            s = dot(key, q, 1, 1)
            edge = jnp.where(allowed, s[lo:hi], NEG)
            s = edge if b == 0 else jnp.concatenate([s[:lo], edge], axis=0)
            e = jnp.exp(s - jnp.max(s, axis=0, keepdims=True))
            p = e * (1.0 / jnp.sum(e, axis=0, keepdims=True))
            gm = gm_ref[h, lo:hi]
            dv = dot(p.astype(BF), gm, 1, 0)
            dp = dot(qkv_ref[2 * heads + h, 0:hi], gm, 1, 1)
            delta = jnp.sum(p * dp, axis=0, keepdims=True)
            ds = (p * (dp - delta)).astype(BF)
            dk = dot(ds, q, 1, 0)
            dq = dot(ds, key, 0, 0) * scale
            dq_ref[lo:hi, h * HD : (h + 1) * HD] = dq
            if b == blocks - 1:
                dk_ref[...] = dk
                dv_ref[...] = dv
            else:
                dk_ref[0:hi] += dk
                dv_ref[0:hi] += dv
        dq_ref[:, part + h * HD : part + (h + 1) * HD] = dk_ref[...]
        value = dv_ref[...].astype(BF)
        lanes = slice(2 * part + h * HD, 2 * part + (h + 1) * HD)
        out_ref[:, lanes] = value
        sum_ref[:, lanes] = jnp.sum(value.astype(F32), axis=0, keepdims=True)
    fetch.wait()
    tables = table_ref[...]
    for g in range(2 * part // 128):
        lanes = slice(g * 128, (g + 1) * 128)
        value = turn(dq_ref[:, lanes], tables, -1).astype(BF)
        out_ref[:, lanes] = value
        sum_ref[:, lanes] = jnp.sum(value.astype(F32), axis=0, keepdims=True)


def attend_back(qkv, grad_all, wout, tables, *first):
    parts, count, _ = qkv.shape
    heads = parts // 3
    width = grad_all.shape[1]
    part = heads * HD
    return pl.pallas_call(
        attend_back_kernel,
        in_specs=[pl.BlockSpec(memory_space=pltpu.VMEM)] * 3
        + [pl.BlockSpec(memory_space=pl.ANY)] * (1 + len(first)),
        out_specs=[pl.BlockSpec(memory_space=pltpu.VMEM)] * 2,
        out_shape=[jax.ShapeDtypeStruct((count, 3 * part), BF), jax.ShapeDtypeStruct((1, 3 * part), F32)],
        scratch_shapes=[
            pltpu.VMEM((heads, LEN, HD), BF),
            pltpu.VMEM((LEN, 2 * part), F32),
            pltpu.VMEM((LEN, HD), F32),
            pltpu.VMEM((LEN, HD), F32),
            pltpu.VMEM((3, LEN, 128), F32),
            pltpu.SemaphoreType.DMA,
        ],
        compiler_params=pltpu.CompilerParams(vmem_limit_bytes=28 * MIB),
        cost_estimate=pl.CostEstimate(
            flops=20 * count * LEN * HD * heads, bytes_accessed=8 * MIB, transcendentals=count * LEN * heads
        ),
        name="attend_back",
    )(qkv, grad_all, wout, tables, *first)


def mlp_back_kernel(grad_ref, slope_ref, wdown_ref, pre_ref, pre_sum_ref, grad_sum_ref):
    grad = grad_ref[...]
    pre = (dot(grad, wdown_ref[...], 1, 1) * slope_ref[...]).astype(BF)
    pre_ref[...] = pre
    pre_sum = jnp.sum(pre.astype(F32), axis=0, keepdims=True)
    grad_sum = jnp.sum(grad.astype(F32), axis=0, keepdims=True)

    @pl.when(pl.program_id(0) == 0)
    def _():
        pre_sum_ref[...] = pre_sum
        grad_sum_ref[...] = grad_sum

    @pl.when(pl.program_id(0) > 0)
    def _():
        pre_sum_ref[...] += pre_sum
        grad_sum_ref[...] += grad_sum


def mlp_back(grad_all, slope, wdown):
    count, width = grad_all.shape
    ff = wdown.shape[0]
    rows = lambda w: pl.BlockSpec((ROWS, w), lambda g: (g, 0))
    return pl.pallas_call(
        mlp_back_kernel,
        grid=(count // ROWS,),
        in_specs=[rows(width), rows(ff), whole(ff, width)],
        out_specs=[rows(ff), whole(1, ff), whole(1, width)],
        out_shape=[
            jax.ShapeDtypeStruct((count, ff), BF), jax.ShapeDtypeStruct((1, ff), F32),
            jax.ShapeDtypeStruct((1, width), F32),
        ],
        compiler_params=pltpu.CompilerParams(vmem_limit_bytes=24 * MIB),
        cost_estimate=pl.CostEstimate(flops=2 * count * width * ff, bytes_accessed=8 * MIB, transcendentals=0),
        name="mlp_back",
    )(grad_all, slope, wdown)


def inputs_back_kernel(
    is_raw, slots, split, which_ref, projected_ref, pre_ref, x_ref, wqkv_ref, win_ref, gain_ref, *refs
):
    out_refs, sum_ref = refs[:-1], refs[-1]
    out_refs = out_refs[-slots:] if split else out_refs[-1:]
    step = pl.program_id(0)
    x = x_ref[...].astype(F32)
    n = normalize(x)[0] if is_raw else x
    first = dot(projected_ref[...], wqkv_ref[...], 1, 0)
    second = dot(pre_ref[...], win_ref[...], 1, 1)
    h = (first * gain_ref[0:1] + second * gain_ref[1:2]).astype(BF)
    column = lambda v: jnp.sum(v, axis=0, keepdims=True)
    sums = jnp.concatenate([column(first * n), column(second * n), column(first), column(second)], axis=0)

    @pl.when(step == 0)
    def _():
        sum_ref[...] = sums

    @pl.when(step > 0)
    def _():
        sum_ref[...] += sums

    if not split:
        out_refs[0][...] = h
        return
    for k in range(slots):

        @pl.when(step == k)
        def _(k=k):
            out_refs[k][...] = h


def inputs_back(which, split, is_raw, projected, pre, x, wqkv, win, gains, *first):
    slots = which.shape[0]
    qkv_width, width = wqkv.shape
    count, ff = x.shape[0], win.shape[1]
    rows = lambda w: pl.BlockSpec((ROWS, w), lambda g, ref: (ref[g], 0))
    outs = [whole(ROWS, width)] * slots if split else [rows(width)]
    shapes = [(ROWS, width)] * slots if split else [(count, width)]
    return pl.pallas_call(
        functools.partial(inputs_back_kernel, is_raw, slots, split),
        grid_spec=pltpu.PrefetchScalarGridSpec(
            num_scalar_prefetch=1,
            grid=(slots,),
            in_specs=[rows(qkv_width), rows(ff), rows(width)]
            + [whole(qkv_width, width), whole(width, ff), whole(2, width)]
            + [pl.BlockSpec(memory_space=pl.ANY)] * len(first),
            out_specs=outs + [whole(4, width)],
        ),
        out_shape=[jax.ShapeDtypeStruct(x, BF) for x in shapes] + [jax.ShapeDtypeStruct((4, width), F32)],
        compiler_params=pltpu.CompilerParams(vmem_limit_bytes=24 * MIB),
        cost_estimate=pl.CostEstimate(
            flops=2 * slots * ROWS * width * (qkv_width + ff), bytes_accessed=4 * MIB, transcendentals=0
        ),
        name="inputs_back",
    )(which, projected, pre, x, wqkv, win, gains, *first)


def place_kernel(side_ref, own_a, own_b, got_a, got_b, *refs):
    out_qkv, out_out, out_in, out_down = refs[-4:]
    first = side_ref[0] == 0

    def both(low_a, low_b, high_a, high_b):
        half, qkv = low_b.shape[0], out_qkv.shape[1]
        out_in[0] = low_a[...].astype(F32)
        out_down[0] = high_a[...].astype(F32)
        out_qkv[0, 0:half] = low_b[...].astype(F32)
        out_qkv[0, half:qkv] = high_b[0 : qkv - half].astype(F32)
        out_out[0] = high_b[qkv - half : half].astype(F32)

    @pl.when(first)
    def _():
        both(own_a, own_b, got_a, got_b)

    @pl.when(jnp.logical_not(first))
    def _():
        both(got_a, got_b, own_a, own_b)


def place(layer, layers, side, own, got, sizes, earlier):
    rows = (sizes[2], (sizes[0] + sizes[1]) // 2)
    arrays, specs = [], []
    tile = 256
    for half in (own, got):
        for k, array in enumerate(half):
            at = 0 if k == 0 or array.shape[0] == rows[1] else rows[0] // rows[1]
            arrays.append(array)
            specs.append(pl.BlockSpec((rows[k], tile), lambda c, ref, at=at: (at, c)))
    width = arrays[0].shape[1]
    more = list(earlier)
    return pl.pallas_call(
        place_kernel,
        grid_spec=pltpu.PrefetchScalarGridSpec(
            num_scalar_prefetch=1,
            grid=(width // tile,),
            in_specs=specs + [pl.BlockSpec(memory_space=pl.ANY)] * len(more),
            out_specs=[pl.BlockSpec((1, r, tile), lambda c, ref: (layer, 0, c)) for r in sizes],
        ),
        out_shape=[jax.ShapeDtypeStruct((layers, r, width), F32) for r in sizes],
        input_output_aliases={5 + k: k for k in range(len(more))},
        compiler_params=pltpu.CompilerParams(vmem_limit_bytes=24 * MIB),
        cost_estimate=pl.CostEstimate(flops=0, bytes_accessed=10 * MIB, transcendentals=0),
        name="place",
    )(side.reshape(1), *arrays, *more)


def weights_kernel(mlp, attention, side_ref, *refs):
    own_ref, other_ref = refs[-2:]
    take = list(refs[: 4 * mlp + 4 * attention])
    low, high = [], []
    if mlp:
        mlp_in, pre, hidden, grad = take[:4]
        take = take[4:]
        for c in range(0, mlp_in.shape[1], ROWS):
            low.append(dot(mlp_in[:, c : c + ROWS], pre[...], 0, 0).astype(BF))
        for c in range(0, hidden.shape[1], ROWS):
            high.append(dot(hidden[:, c : c + ROWS], grad[...], 0, 0).astype(BF))
    if attention:
        projected, attn_in, mixed, grad = take
        cut = (projected.shape[1] + mixed.shape[1]) // 2
        low.append(dot(projected[:, :cut], attn_in[...], 0, 0).astype(BF))
        high.append(dot(projected[:, cut:], attn_in[...], 0, 0).astype(BF))
        high.append(dot(mixed[...], grad[...], 0, 0).astype(BF))

    def write(ref, pieces):
        at = 0
        for piece in pieces:
            ref[at : at + piece.shape[0]] = piece
            at += piece.shape[0]

    @pl.when(side_ref[0] == 0)
    def _():
        write(own_ref, low)
        write(other_ref, high)

    @pl.when(side_ref[0] != 0)
    def _():
        write(own_ref, high)
        write(other_ref, low)


def weights_back(side, mlp=(), attention=(), first=()):
    arrays = [*mlp, *attention]
    width = arrays[1].shape[1]
    rows = (mlp[0].shape[1] if mlp else 0) + ((attention[0].shape[1] + attention[2].shape[1]) // 2 if attention else 0)
    return pl.pallas_call(
        functools.partial(weights_kernel, bool(mlp), bool(attention)),
        in_specs=[pl.BlockSpec(memory_space=pltpu.SMEM)]
        + [pl.BlockSpec(memory_space=pltpu.VMEM)] * len(arrays)
        + [pl.BlockSpec(memory_space=pl.ANY)] * len(first),
        out_specs=[pl.BlockSpec(memory_space=pltpu.VMEM)] * 2,
        out_shape=[jax.ShapeDtypeStruct((rows, width), BF)] * 2,
        compiler_params=pltpu.CompilerParams(vmem_limit_bytes=16 * MIB),
        cost_estimate=pl.CostEstimate(
            flops=4 * rows * width * arrays[0].shape[0], bytes_accessed=6 * MIB, transcendentals=0
        ),
        name="weights_back",
    )(side.reshape(1), *arrays, *first)


def quarters_kernel(which_ref, own_ref, got_ref, *out_refs):
    step = pl.program_id(0)
    total = (own_ref[...].astype(F32) + got_ref[...].astype(F32)).astype(BF)
    for k in range(4):

        @pl.when(step == k)
        def _(k=k):
            out_refs[k][...] = total


def quarters(which, own, got):
    rows, width = own.shape[0] // 4, own.shape[1]
    spec = pl.BlockSpec((rows, width), lambda g, ref: (ref[g], 0))
    return pl.pallas_call(
        quarters_kernel,
        grid_spec=pltpu.PrefetchScalarGridSpec(
            num_scalar_prefetch=1,
            grid=(4,),
            in_specs=[spec, spec],
            out_specs=[whole(rows, width)] * 4,
        ),
        out_shape=[jax.ShapeDtypeStruct((rows, width), BF)] * 4,
        compiler_params=pltpu.CompilerParams(vmem_limit_bytes=16 * MIB),
        cost_estimate=pl.CostEstimate(flops=0, bytes_accessed=6 * MIB, transcendentals=0),
        name="quarters",
    )(which, own, got)


def forward_norm_kernel(x_ref, branch_ref, out_ref, down_ref, stream_ref, n_ref):
    stream = x_ref[...].astype(F32) + branch_ref[...].astype(F32) + out_ref[...] + down_ref[...]
    stream_ref[...] = stream
    n_ref[...] = normalize(stream)[0].astype(BF)


def forward_norm(x, branch, out_bias, down_bias):
    here = pl.BlockSpec(memory_space=pltpu.VMEM)
    return pl.pallas_call(
        forward_norm_kernel,
        in_specs=[here] * 4,
        out_specs=[here] * 2,
        out_shape=[jax.ShapeDtypeStruct(x.shape, F32), jax.ShapeDtypeStruct(x.shape, BF)],
        compiler_params=pltpu.CompilerParams(vmem_limit_bytes=12 * MIB),
        cost_estimate=pl.CostEstimate(flops=0, bytes_accessed=2 * MIB, transcendentals=0),
        name="forward_norm",
    )(x, branch, out_bias.reshape(1, -1), down_bias.reshape(1, -1))


def backward_norm_kernel(x_ref, h_ref, grad_ref, *refs):
    n, scale = normalize(x_ref[...].astype(F32))
    h = h_ref[...].astype(F32)
    mean = lambda v: jnp.mean(v, axis=-1, keepdims=True)
    grad = grad_ref[...].astype(F32) + scale * (h - mean(h) - n * mean(h * n))
    refs[-2][...] = grad
    refs[-1][...] = grad.astype(BF)


def backward_norm(x, h, grad, first=()):
    here = pl.BlockSpec(memory_space=pltpu.VMEM)
    return pl.pallas_call(
        backward_norm_kernel,
        in_specs=[here] * 3 + [pl.BlockSpec(memory_space=pl.ANY)] * len(first),
        out_specs=[here] * 2,
        out_shape=[jax.ShapeDtypeStruct(x.shape, F32), jax.ShapeDtypeStruct(x.shape, BF)],
        compiler_params=pltpu.CompilerParams(vmem_limit_bytes=12 * MIB),
        cost_estimate=pl.CostEstimate(flops=0, bytes_accessed=2 * MIB, transcendentals=0),
        name="backward_norm",
    )(x, h, grad, *first)


def after_kernel(count, *refs):
    for k in range(count):
        refs[len(refs) - count + k][...] = refs[k][...]


def after(arrays, *first):
    here = pl.BlockSpec(memory_space=pltpu.VMEM)
    return pl.pallas_call(
        functools.partial(after_kernel, len(arrays)),
        in_specs=[here] * len(arrays) + [pl.BlockSpec(memory_space=pl.ANY)] * len(first),
        out_specs=[here] * len(arrays),
        out_shape=[jax.ShapeDtypeStruct(x.shape, x.dtype) for x in arrays],
        cost_estimate=pl.CostEstimate(flops=0, bytes_accessed=MIB, transcendentals=0),
        compiler_params=pltpu.CompilerParams(vmem_limit_bytes=8 * MIB),
        name="after",
    )(*arrays, *first)


UP = [(0, 1), (1, 2), (2, 3)]
DOWN = [(1, 0), (2, 1), (3, 2)]


def send(x, pairs):
    return lax.ppermute(x, "tensor", pairs)


ENDS = [(0, 3), (3, 0)]


def gather_near(x):
    return send(x, UP), send(x, DOWN), send(x, ENDS)


def gather_rest(x, near):
    below, above, far = near
    a = send(above, [(1, 0), (2, 1)])
    c = send(below, [(2, 3), (1, 2)])
    i = lax.axis_index("tensor")
    pick = lambda *four: lax.select_n(jnp.broadcast_to(i, x.shape), *four)
    return jnp.concatenate(
        [pick(x, below, c, far), pick(above, x, below, c), pick(a, above, x, below), pick(far, a, above, x)], axis=0
    )


def gather_rows(x):
    return gather_rest(x, gather_near(x))


def whole_rows(x):
    return lax.all_gather(x, "tensor", axis=0, tiled=True)


def own_sum(x):
    return lax.psum_scatter(x, "tensor", scatter_dimension=0, tiled=True)


def partner(x, axis, bit):
    return lax.ppermute(x, axis, [(k, k ^ bit) for k in range(lax.axis_size(axis))])


def plane_send(own, other):
    k = (lax.axis_index("dp") // 2) % 4
    which = jnp.stack([k ^ j for j in range(4)])
    return quarters(which, own, partner(other, "dp", 1))


def plane_sum(four):
    size = lax.axis_size("dp")
    got = [partner(four[j], "dp", 2 * j) for j in (1, 2, 3)]
    own = sum(t.astype(F32) for t in [four[0]] + got).astype(BF)
    if size > 8:
        groups = [[g * 8 + k for g in range(size // 8)] for k in range(8)]
        own = lax.psum(own, "dp", axis_index_groups=groups)
    return own


def plane_gather(own):
    k = (lax.axis_index("dp") // 2) % 4
    four = [own] + [partner(own, "dp", 2 * j) for j in (1, 2, 3)]
    return jnp.concatenate([lax.select_n(jnp.broadcast_to(k ^ j, own.shape), *four) for j in range(4)], axis=0)


def sum_small(x, axis):
    size = lax.axis_size(axis)
    if size & (size - 1):
        return lax.psum(x, axis)
    bit = 1
    while bit < size:
        x = x + partner(x, axis, bit)
        bit *= 2
    return x


def body(tokens, cotangent, norm_gain, norm_shift, w_qkv, b_qkv, w_out, b_out, w_in, b_in, w_down, b_down):
    layers = w_qkv.shape[0]
    width = tokens.shape[1]
    wqkv = w_qkv.transpose(0, 2, 3, 1).reshape(layers, -1, width)
    sizes = (wqkv.shape[1], w_out.shape[1], width, w_down.shape[1])
    i = lax.axis_index("tensor")
    in_order = jnp.arange(4, dtype=jnp.int32)
    far_blocks = jnp.stack([(i + 2) % 4, 3 - i])
    near_blocks = jnp.stack([i ^ 1, i])
    tables = rope_tables()

    stream = tokens
    gathered = gather_rows(tokens)
    grad_all = whole_rows(cotangent)
    kept = []
    for l in range(layers):
        last = l == layers - 1
        if l > 0:
            gathered = whole_rows(n_own)
        attn_in, mlp_in, qkv, hidden, slope = project(
            gathered, l == 0, norm_gain[l], norm_shift[l], tables, wqkv[l], b_qkv[l], w_in[l], b_in[l]
        )
        branch, mixed = attend(in_order, qkv, hidden, w_out[l], w_down[l])
        kept.append((stream, gathered, attn_in, mlp_in, qkv, hidden, slope, mixed))
        if not last:
            stream, n_own = forward_norm(stream, own_sum(branch), b_out[l], b_down[l])

    grad_stream = cotangent
    biases, norms = [None] * layers, [None] * layers
    side = lax.axis_index("dp") % 2
    placed = ()
    wait_gather, wait_near, wait_attend, wait_inputs = (), (), (), ()
    for l in reversed(range(layers)):
        stream_in, gathered, attn_in, mlp_in, qkv, hidden, slope, mixed = kept[l]
        final = l == 0
        if l < layers - 1:
            below, above, far = gather_near(grad_low)
            below, above = after([below, above], *wait_near)
            grad_all = gather_rest(grad_low, (below, above, far))
        if l == max(layers - 2, 0):
            late = own_sum(after([branch], grad_all)[0])
        grad_pre, pre_sum, grad_sum = mlp_back(grad_all, slope, w_down[l])
        mlp = (mlp_in, grad_pre, hidden, grad_all)
        if final:
            mlp_own, mlp_other = weights_back(side, mlp=mlp)
            wait_attend += (mlp_other,)
        grad_projected, projected_sum = attend_back(qkv, grad_all, w_out[l], tables, mixed, *wait_attend)
        if final:
            mlp_four = plane_send(mlp_own, mlp_other)
            wait_inputs += (mlp_four[1],)
        h, norms[l] = inputs_back(
            in_order, False, final, grad_projected, grad_pre, gathered, wqkv[l], w_in[l], norm_gain[l], *wait_inputs
        )
        h_own = own_sum(h)
        attention = (grad_projected, attn_in, mixed, grad_all)
        biases[l] = (projected_sum[0], pre_sum[0], grad_sum[0])
        if final:
            attention_own, attention_other = weights_back(side, attention=attention, first=(h,))
            attention_four = plane_send(attention_own, attention_other)
            own = [plane_gather(plane_sum(mlp_four)), plane_gather(plane_sum(attention_four))]
            got = [partner(x, "dp", 1) for x in own]
            norms[l] = after([norms[l]], attention_other, placed[1])[0]
            placed = place(l, layers, side, own, got, sizes, placed)
            wait_gather = ()
        else:
            own, other = weights_back(side, mlp=mlp, attention=attention, first=(h,))
            four = plane_send(own, other)
            wait_gather = (four[1],)
            own = plane_sum(four)
            wait_near = (own,)
            own = plane_gather(own)
            wait_attend = (own,)
            got = partner(own, "dp", 1)
            placed = place(l, layers, side, (own, own), (got, got), sizes, placed)
        grad_stream, grad_low = backward_norm(stream_in, h_own, grad_stream, wait_gather)

    result = stream + late.astype(F32) + b_out[layers - 1] + b_down[layers - 1]
    norm_sums = sum_small(jnp.concatenate(norms, axis=0), "tensor")
    part = wqkv.shape[1]
    pad = lambda v: jnp.pad(v, (0, width - v.shape[0]))[None]
    small = sum_small(jnp.concatenate([norm_sums] + [pad(v) for three in biases for v in three], axis=0), "dp")
    norm_sums = small[: 4 * layers].reshape(layers, 4, width)
    rest = small[4 * layers :].reshape(layers, 3, width)
    g_qkv, g_out, g_in, g_down = placed
    g_qkv = g_qkv.reshape(layers, 3, part // 3, width).transpose(0, 3, 1, 2)
    gb_qkv = rest[:, 0, :part].reshape(layers, 3, part // 3)
    gb_in = rest[:, 1, : b_in.shape[1]]
    gb_out = rest[:, 2]
    return (
        result, grad_stream, norm_sums[:, 0:2], norm_sums[:, 2:4],
        g_qkv, gb_qkv, g_out, gb_out, g_in, gb_in, g_down, gb_out,
    )


def solution(mesh):
    rows = P(("dp", "tensor"), None)
    specs = (
        P(None, None, None, "tensor"), P(None, None, "tensor"), P(None, "tensor", None), P(),
        P(None, None, "tensor"), P(None, "tensor"), P(None, "tensor", None), P(),
    )
    both = (rows, rows, P(), P()) + specs
    return jax.shard_map(body, mesh=mesh, in_specs=both, out_specs=both, check_vma=False)
```
